128 devices in a mesh: gx: 4 (over z), gy: 32 (over y, x, core).
Axes of the slice: x: 4, y: 4, z: 4, core: 2. Of those that a mesh axis runs over, the one named last changes fastest.
Arguments:
- token_ids: int32 [128, 3], P(('gx', 'gy')), may hold values from 0 to 383
- mem_lengths: int32 [128], P(('gx', 'gy')), may hold values from 64 to 256, as said below
- embed_table: bfloat16 [384, 4672], replicated, may hold values from -1.796875 to 1.796875
- w_qkv: bfloat16 [1, 4672, 3, 4096], P(None, 'gx', None, 'gy'), may hold values from -0.09375 to 0.09375
- w_self_out: bfloat16 [1, 4096, 4672], P(None, 'gx', 'gy'), may hold values from -0.09375 to 0.09375
- w_cross_q: bfloat16 [1, 4672, 4096], P(None, 'gx', 'gy'), may hold values from -0.09375 to 0.09375
- w_cross_out: bfloat16 [1, 4096, 4672], P(None, 'gx', 'gy'), may hold values from -0.09375 to 0.09375
- w_in: bfloat16 [1, 4672, 2, 12352], P(None, 'gx', None, 'gy'), may hold values from -0.09375 to 0.09375
- w_out: bfloat16 [1, 12352, 4672], P(None, 'gx', 'gy'), may hold values from -0.0546875 to 0.0546875
- lm_head: bfloat16 [4672, 384], P('gx', 'gy'), may hold values from -0.09375 to 0.09375
- gain_self: float32 [1, 4672], replicated, may hold values from 0.1 to 1.9
- gain_cross: float32 [1, 4672], replicated, may hold values from 0.1 to 1.9
- gain_ffn: float32 [1, 4672], replicated, may hold values from 0.1 to 1.9
- gain_final: float32 [4672], replicated, may hold values from 0.1 to 1.9
- self_keys: bfloat16 [1, 128, 128, 4096], P(None, ('gx', 'gy')), may hold values from -6 to 6
- self_values: bfloat16 [1, 128, 128, 4096], P(None, ('gx', 'gy')), may hold values from -15 to 15
- cross_keys: bfloat16 [1, 128, 256, 4096], P(None, ('gx', 'gy')), may hold values from -6 to 6
- cross_values: bfloat16 [1, 128, 256, 4096], P(None, ('gx', 'gy')), may hold values from -15 to 15
Outputs:
- logits: bfloat16 [3, 128, 384], P(None, ('gx', 'gy'))
The draws below stay inside these ranges and needn't reach their ends.
Inputs may be any that keep to these rules, and one draw needn't show every extreme that they name: `mem_lengths`: some line has all 256 positions valid in every draw.
All inputs are finite; a program needn't handle non-finite values.
Results may differ from the reference program's by a relative error of at most 0.025.
Values may be sent and summed in bfloat16 or wider, within the bound.
No kernel may reach another device: no remote copies, remote signals or barrier semaphores. Data moves between devices by JAX's collectives and lax.ppermute only.
A program may use at most 192 MiB of HBM per device.

```python
import jax
import jax.numpy as jnp
from jax import lax

D = 4672
HEADS = 64
HEAD_DIM = 64
FF = 12352
VOCAB = 384
PREFIX = 128
MEM = 256
LAYERS = 1
STEPS = 3
INNER = 4096
LINES = 128


def draw_mem_lengths(key, part):
    key = jax.random.fold_in(key, 11)
    base = jax.random.randint(jax.random.fold_in(key, 1), (LINES,), MEM // 4, MEM + 1)
    offset = jax.random.randint(jax.random.fold_in(key, 2), (), 0, 5)
    full_line = jnp.arange(LINES, dtype=jnp.int32) % 5 == offset
    return jnp.where(full_line, MEM, base).astype(jnp.int32)


def set_ends(array, stream_key, smallest, largest):
    index_at = [jax.random.randint(jax.random.fold_in(stream_key, axis), (), 0, length) for axis, length in enumerate(array.shape)]
    widest = array.shape.index(max(array.shape))
    beside = index_at[:widest] + [(index_at[widest] + 1) % array.shape[widest]] + index_at[widest + 1:]
    return array.at[tuple(index_at)].set(smallest).at[tuple(beside)].set(largest)


def steps_of(own_key, dims, split, low, high):
    def one(dim, shards_of):
        draws = jax.random.uniform(jax.random.fold_in(jax.random.fold_in(own_key, 6), dim), (shards_of,), jnp.float32, low / len(split), high / len(split))
        return jnp.repeat(jnp.exp(draws), dims[dim] // shards_of).reshape((-1,) + (1,) * (len(dims) - dim - 1))

    level = one(*split[0])
    for cut in split[1:]:
        level = level * one(*cut)
    return level


def gaussian(stream_key, shape, scale, most, split=(), kind=jnp.bfloat16):
    level = steps_of(stream_key, shape, split, -0.22, 0.18) if split else 1.0
    drawn = jax.random.normal(stream_key, shape, jnp.float32) * scale * level
    return jnp.minimum(jnp.maximum(drawn, -most), most).astype(kind)


def setup_inputs(seed: int = 0) -> dict:
    key_list = jax.random.split(jax.random.key(seed), 19)
    token_ids = set_ends(jax.random.randint(key_list[0], (LINES, STEPS), 0, VOCAB), jax.random.fold_in(key_list[0], 1), 0, VOCAB - 1).astype(jnp.int32)
    mem_lengths = draw_mem_lengths(jax.random.fold_in(key_list[18], 71), 0)
    embed_table = gaussian(key_list[2], (VOCAB, D), 0.3, 1.796875)
    w_qkv = gaussian(key_list[3], (LAYERS, D, 3, INNER), D ** -0.5, 0.09375, ((1, 4), (3, 32)))
    w_self_out = gaussian(key_list[4], (LAYERS, INNER, D), INNER ** -0.5, 0.09375, ((1, 4), (2, 32)))
    w_cross_q = gaussian(key_list[5], (LAYERS, D, INNER), D ** -0.5, 0.09375, ((1, 4), (2, 32)))
    w_cross_out = gaussian(key_list[6], (LAYERS, INNER, D), INNER ** -0.5, 0.09375, ((1, 4), (2, 32)))
    w_in = gaussian(key_list[7], (LAYERS, D, 2, FF), D ** -0.5, 0.09375, ((1, 4), (3, 32)))
    w_out = gaussian(key_list[8], (LAYERS, FF, D), FF ** -0.5, 0.0546875, ((1, 4), (2, 32)))
    lm_head = gaussian(key_list[9], (D, VOCAB), D ** -0.5, 0.09375, ((0, 4), (1, 32)))
    gain_self = jnp.clip(1.0 + 0.18 * jax.random.normal(key_list[10], (LAYERS, D), jnp.float32), 0.1, 1.9)
    gain_cross = jnp.clip(1.0 + 0.18 * jax.random.normal(key_list[11], (LAYERS, D), jnp.float32), 0.1, 1.9)
    gain_ffn = jnp.clip(1.0 + 0.18 * jax.random.normal(key_list[12], (LAYERS, D), jnp.float32), 0.1, 1.9)
    gain_final = jnp.clip(1.0 + 0.18 * jax.random.normal(key_list[13], (D,), jnp.float32), 0.1, 1.9)
    self_keys = gaussian(key_list[14], (LAYERS, LINES, PREFIX, INNER), 1.0, 6.0, ((1, 128),))
    self_values = gaussian(key_list[15], (LAYERS, LINES, PREFIX, INNER), 3.0, 15.0, ((1, 128),))
    cross_keys = gaussian(key_list[16], (LAYERS, LINES, MEM, INNER), 1.0, 6.0, ((1, 128),))
    cross_values = gaussian(key_list[17], (LAYERS, LINES, MEM, INNER), 3.0, 15.0, ((1, 128),))
    return {"token_ids": token_ids, "mem_lengths": mem_lengths, "embed_table": embed_table, "w_qkv": w_qkv, "w_self_out": w_self_out, "w_cross_q": w_cross_q, "w_cross_out": w_cross_out, "w_in": w_in, "w_out": w_out, "lm_head": lm_head, "gain_self": gain_self, "gain_cross": gain_cross, "gain_ffn": gain_ffn, "gain_final": gain_final, "self_keys": self_keys, "self_values": self_values, "cross_keys": cross_keys, "cross_values": cross_values}


def normalize(state, gain):
    scale = lax.rsqrt(lax.optimization_barrier(jnp.mean(state * state, axis=-1, keepdims=True)) + 1e-06)
    return (state * scale * gain).astype(jnp.bfloat16)

def project(vector, weight):
    flat = weight.reshape(weight.shape[0], -1)
    return jnp.dot(vector, flat, preferred_element_type=jnp.float32).astype(jnp.bfloat16)

def attend_self(query, cache_k, cache_v, fresh_k, fresh_v):
    keys = jnp.concatenate([cache_k, fresh_k], axis=0).reshape(-1, HEADS, HEAD_DIM).astype(jnp.float32)
    values = jnp.concatenate([cache_v, fresh_v], axis=0).reshape(-1, HEADS, HEAD_DIM).astype(jnp.float32)
    scores = 0.125 * jnp.einsum('hd,phd->hp', query.astype(jnp.float32), keys)
    weights = jax.nn.softmax(scores, axis=-1).astype(jnp.bfloat16).astype(jnp.float32)
    return jnp.einsum('hp,phd->hd', weights, values).astype(jnp.bfloat16)

def attend_cross(query, keys, values, length):
    keys = keys.reshape(-1, HEADS, HEAD_DIM).astype(jnp.float32)
    values = values.reshape(-1, HEADS, HEAD_DIM).astype(jnp.float32)
    scores = 0.125 * jnp.einsum('hd,phd->hp', query.astype(jnp.float32), keys)
    valid = jnp.arange(keys.shape[0], dtype=jnp.int32) < length
    scores = jnp.where(valid[None, :], scores, -1e+30)
    weights = jax.nn.softmax(scores, axis=-1).astype(jnp.bfloat16).astype(jnp.float32)
    return jnp.einsum('hp,phd->hd', weights, values).astype(jnp.bfloat16)

def reference(token_ids, mem_lengths, embed_table, w_qkv, w_self_out, w_cross_q, w_cross_out, w_in, w_out, lm_head, gain_self, gain_cross, gain_ffn, gain_final, self_keys, self_values, cross_keys, cross_values):
    lines = token_ids.shape[0]
    fresh_keys = [[] for layer in range(LAYERS)]
    fresh_values = [[] for layer in range(LAYERS)]
    outputs = []
    for step in range(STEPS):
        state = embed_table[token_ids[:, step]].astype(jnp.float32)
        for layer in range(LAYERS):
            triple = project(normalize(state, gain_self[layer]), w_qkv[layer]).reshape(lines, 3, INNER)
            query = triple[:, 0].reshape(lines, HEADS, HEAD_DIM)
            fresh_keys[layer].append(triple[:, 1])
            fresh_values[layer].append(triple[:, 2])
            new_k = jnp.stack(fresh_keys[layer], axis=1)
            new_v = jnp.stack(fresh_values[layer], axis=1)
            attended = lax.map(lambda parts: attend_self(*parts), (query, self_keys[layer], self_values[layer], new_k, new_v))
            state = state + project(attended.reshape(lines, INNER), w_self_out[layer]).astype(jnp.float32)
            query = project(normalize(state, gain_cross[layer]), w_cross_q[layer]).reshape(lines, HEADS, HEAD_DIM)
            attended = lax.map(lambda parts: attend_cross(*parts), (query, cross_keys[layer], cross_values[layer], mem_lengths))
            state = state + project(attended.reshape(lines, INNER), w_cross_out[layer]).astype(jnp.float32)
            gate_up = project(normalize(state, gain_ffn[layer]), w_in[layer]).reshape(lines, 2, FF).astype(jnp.float32)
            hidden = (jax.nn.gelu(gate_up[:, 0], approximate=True) * gate_up[:, 1]).astype(jnp.bfloat16)
            state = state + project(hidden, w_out[layer]).astype(jnp.float32)
        outputs.append(project(normalize(state, gain_final), lm_head))
    return jnp.stack(outputs, axis=0)
```

```python
import jax
import jax.numpy as jnp
from jax import lax
from jax.sharding import Mesh, PartitionSpec as P

HEADS = 64
HEAD_DIM = 64
STEPS = 3
Z, Y, X, C = 4, 4, 4, 2
XC = X * C
PLANE = Z * XC
ROWS = PLANE * STEPS
BF = jnp.bfloat16
F32 = jnp.float32


def swap(pieces, axes):
    return lax.all_to_all(pieces, axes, 0, 0, tiled=True)


def spread(block, count, axes):
    return swap(jnp.broadcast_to(block[None], (count,) + block.shape), axes)


def dot(a, b):
    return jnp.dot(a, b, preferred_element_type=F32)


def dot_t(a, b):
    return lax.dot_general(a, b, (((1,), (1,)), ((), ())), preferred_element_type=F32)


def two_halves(value):
    high = value.astype(BF)
    return high, (value - high.astype(F32)).astype(BF)


def head_mask(inner):
    heads = lax.broadcasted_iota(jnp.int32, (HEADS, inner), 0)
    owner = lax.broadcasted_iota(jnp.int32, (HEADS, inner), 1) // HEAD_DIM
    return heads == owner


def by_head(query, mask):
    spread_out = jnp.where(mask[None], query[:, None, :], jnp.zeros((), BF))
    return spread_out.reshape(STEPS * HEADS, -1)


def own_heads(mixed, mask):
    inner = mask.shape[1]
    kept = jnp.where(mask[None], mixed.reshape(STEPS, HEADS, inner), 0.0)
    return jnp.sum(kept, axis=1).astype(BF)


def attend_self(query, cache_k, cache_v, fresh_k, fresh_v):
    mask = head_mask(query.shape[1])
    wide = by_head(query, mask)
    prefix = cache_k.shape[0]
    step_of = lax.broadcasted_iota(jnp.int32, (STEPS, HEADS, STEPS), 0).reshape(-1, STEPS)
    key_of = lax.broadcasted_iota(jnp.int32, (STEPS * HEADS, STEPS), 1)
    scores_new = jnp.where(key_of <= step_of, 0.125 * dot_t(wide, fresh_k), -jnp.inf)
    scores = jnp.concatenate([0.125 * dot_t(wide, cache_k), scores_new], axis=1)
    weights = jax.nn.softmax(scores, axis=-1).astype(BF)
    mixed = dot(weights[:, :prefix], cache_v) + dot(weights[:, prefix:], fresh_v)
    return own_heads(mixed, mask)


def attend_cross(query, keys, values, length):
    mask = head_mask(query.shape[1])
    scores = 0.125 * dot_t(by_head(query, mask), keys)
    valid = lax.broadcasted_iota(jnp.int32, scores.shape, 1) < length
    weights = jax.nn.softmax(jnp.where(valid, scores, -1e30), axis=-1).astype(BF)
    return own_heads(dot(weights, values), mask)


def to_plane(attended):
    quarters = attended.reshape(STEPS, Z, -1).transpose(1, 0, 2)
    pieces = jnp.broadcast_to(quarters[:, None], (Z, XC) + quarters.shape[1:])
    got = swap(pieces.reshape((PLANE,) + quarters.shape[1:]), ("z", "x", "c"))
    return got.reshape(ROWS, -1)


def blocks_of(rows, weights):
    return jnp.stack([dot_t(rows, weights[i]).astype(BF) for i in range(Y)])


def to_quarter(state):
    got = spread(state.astype(BF), XC, ("x", "c"))
    return got.transpose(1, 0, 2).reshape(ROWS, -1)


def body(
    token_ids,
    mem_lengths,
    embed_table,
    w_qkv,
    w_self_out,
    w_cross_q,
    w_cross_out,
    w_in,
    w_out,
    lm_head,
    gain_self,
    gain_cross,
    gain_ffn,
    gain_final,
    self_keys,
    self_values,
    cross_keys,
    cross_values,
):
    z, y = lax.axis_index("z"), lax.axis_index("y")
    x, c = lax.axis_index("x"), lax.axis_index("c")
    width = embed_table.shape[1]
    vocab = embed_table.shape[0]
    quarter = width // Z
    block = quarter // XC

    def part_of(gain):
        return lax.dynamic_slice_in_dim(gain, z * quarter, quarter)

    self_out = lax.all_gather(w_self_out[0].T, "y")
    cross_q = lax.all_gather(w_cross_q[0], "y")
    cross_out = lax.all_gather(w_cross_out[0].T, "y")
    flip = [(i * Y + j, j * Y + i) for i in range(Z) for j in range(Y)]
    down = lax.all_gather(lax.ppermute(w_out[0].T, ("z", "y"), flip), "z")
    head = lax.all_gather(lm_head.T, "y")

    tokens = spread(token_ids, Y * XC, ("y", "x", "c"))
    tokens = spread(tokens.reshape(Y * XC, STEPS), Z, "z").reshape(Z, Y, XC, STEPS)
    vocab_range = jnp.arange(vocab, dtype=jnp.int32)
    pick_all = (tokens.reshape(-1)[:, None] == vocab_range[None, :]).astype(BF)
    plane_tokens = lax.dynamic_index_in_dim(tokens, y, 1, keepdims=False).reshape(-1)
    pick_plane = (plane_tokens[:, None] == vocab_range[None, :]).astype(BF)
    start = z * quarter + (x * C + c) * block
    state = dot(pick_plane, lax.dynamic_slice_in_dim(embed_table, start, block, axis=1))

    table = embed_table.astype(F32)
    scale = lax.rsqrt(jnp.mean(table * table, axis=-1, keepdims=True) + 1e-06)
    own = lax.dynamic_slice_in_dim(embed_table, z * quarter, quarter, axis=1).astype(F32)
    own = (own * scale * part_of(gain_self[0])[None]).astype(BF)
    triple = jnp.concatenate([dot(own, w_qkv[0, :, i]).astype(BF) for i in range(3)], axis=1)
    triple = dot(pick_all, triple).astype(BF)
    triple = swap(triple.reshape(Z, ROWS, -1), "z").astype(F32).sum(axis=0).astype(BF)
    triple = swap(triple.reshape(Y * XC, STEPS, -1), ("y", "x", "c"))
    triple = triple.reshape(Y * XC, STEPS, 3, -1).transpose(2, 1, 0, 3).reshape(3, STEPS, -1)
    attended = attend_self(triple[0], self_keys[0, 0], self_values[0, 0], triple[1], triple[2])

    parts = swap(blocks_of(to_plane(attended), self_out), "z")
    state = state + parts.astype(F32).sum(axis=0).astype(BF).astype(F32)

    rows = to_quarter(state).astype(F32)
    squares = two_halves(jnp.sum(rows * rows, axis=1, keepdims=True))
    rows = (rows * part_of(gain_cross[0])[None]).astype(BF)
    tail = jnp.concatenate(squares + (jnp.zeros((ROWS, 126), BF),), axis=1)
    parts = jnp.concatenate([dot(rows, cross_q[i]).astype(BF) for i in range(Y)] + [tail], axis=1)
    parts = swap(parts.reshape(PLANE, STEPS, -1), ("z", "x", "c"))
    parts = parts.astype(F32).reshape(Z, XC, STEPS, -1).sum(axis=0)
    inner = parts.shape[2] - 128
    scale = lax.rsqrt((parts[0, :, inner] + parts[0, :, inner + 1]) / width + 1e-06)
    query = (parts[:, :, :inner] * scale[None, :, None]).astype(BF)
    query = query.reshape(XC, STEPS, Y, -1).transpose(1, 2, 0, 3).reshape(STEPS, -1)
    attended = attend_cross(query, cross_keys[0, 0], cross_values[0, 0], mem_lengths[0])

    parts = swap(blocks_of(to_plane(attended), cross_out), "z")
    state = state + parts.astype(F32).sum(axis=0).astype(BF).astype(F32)

    near = spread(state.astype(BF), Y * X, ("y", "x"))
    far = lax.ppermute(near, "c", [(0, 1), (1, 0)])
    both = lax.dynamic_slice_in_dim(jnp.stack([near, far, near]), c, C, axis=0)
    rows = both.reshape(C, Y, X, ROWS, block).transpose(1, 3, 2, 0, 4).reshape(Y * ROWS, quarter)
    rows = rows.astype(F32)
    squares = two_halves(jnp.sum(rows * rows, axis=1, keepdims=True))
    rows = (rows * part_of(gain_ffn[0])[None]).astype(BF)
    gate = dot(rows, w_in[0, :, 0]).astype(BF)
    up = dot(rows, w_in[0, :, 1]).astype(BF)
    parts = jnp.concatenate((gate, up) + squares, axis=1)
    parts = swap(parts.reshape(Z, ROWS, -1), "z").astype(F32).sum(axis=0)
    hidden = gate.shape[1]
    scale = lax.rsqrt((parts[:, 2 * hidden] + parts[:, 2 * hidden + 1]) / width + 1e-06)[:, None]
    gate = (parts[:, :hidden] * scale).astype(BF).astype(F32)
    up = (parts[:, hidden : 2 * hidden] * scale).astype(BF).astype(F32)
    hidden = (jax.nn.gelu(gate, approximate=True) * up).astype(BF)

    parts = blocks_of(to_quarter(hidden), down)
    got = []
    for shift in range(Y):
        piece = lax.dynamic_index_in_dim(parts, (y + shift) % Y, 0, keepdims=False)
        pairs = [(i * Y + j, ((j + shift) % Y) * Y + i) for i in range(Z) for j in range(Y)]
        got.append(lax.ppermute(piece, ("z", "y"), pairs).astype(F32))
    state = state + (got[0] + got[1] + got[2] + got[3]).astype(BF).astype(F32)

    rows = to_quarter(state).astype(F32)
    squares = two_halves(jnp.sum(rows * rows, axis=1, keepdims=True))
    rows = (rows * part_of(gain_final)[None]).astype(BF)
    parts = [dot_t(rows, head[i]).astype(BF) for i in range(Y)]
    parts = jnp.concatenate(parts + list(squares), axis=1)
    parts = swap(parts.reshape(PLANE, STEPS, -1), ("z", "x", "c"))
    parts = parts.astype(F32).reshape(Z, XC, STEPS, -1).sum(axis=0)
    inner = parts.shape[2] - 2
    scale = lax.rsqrt((parts[0, :, inner] + parts[0, :, inner + 1]) / width + 1e-06)
    logits = (parts[:, :, :inner] * scale[None, :, None]).astype(BF)
    logits = logits.reshape(XC, STEPS, Y, -1).transpose(1, 2, 0, 3)
    return logits.reshape(STEPS, 1, -1)


def solution(mesh):
    fine = Mesh(mesh.devices.reshape(Z, Y, X, C), ("z", "y", "x", "c"))
    lines = ("z", "y", "x", "c")
    columns = ("y", "x", "c")
    placed = (
        P(lines, None),
        P(lines),
        P(),
        P(None, "z", None, columns),
        P(None, "z", columns),
        P(None, "z", columns),
        P(None, "z", columns),
        P(None, "z", None, columns),
        P(None, "z", columns),
        P("z", columns),
        P(),
        P(),
        P(),
        P(),
        P(None, lines, None, None),
        P(None, lines, None, None),
        P(None, lines, None, None),
        P(None, lines, None, None),
    )
    return jax.shard_map(
        body, mesh=fine, in_specs=placed, out_specs=P(None, lines, None), check_vma=False
    )
```

```python
import jax
import jax.numpy as jnp
from jax import lax
from jax.experimental import pallas as pl
from jax.experimental.pallas import tpu as pltpu
from jax.sharding import Mesh, PartitionSpec as P

HEADS = 64
HEAD_DIM = 64
STEPS = 3
Z, Y, X, C = 4, 4, 4, 2
XC = X * C
PLANE = Z * XC
ROWS = PLANE * STEPS
BF = jnp.bfloat16
F32 = jnp.float32


def swap(pieces, axes):
    return lax.all_to_all(pieces, axes, 0, 0, tiled=True)


def spread(block, count, axes):
    return swap(jnp.broadcast_to(block[None], (count,) + block.shape), axes)


def dot(a, b):
    return jnp.dot(a, b, preferred_element_type=F32)


def dot_t(a, b):
    return lax.dot_general(a, b, (((1,), (1,)), ((), ())), preferred_element_type=F32)


def two_halves(value):
    high = value.astype(BF)
    return high, (value - high.astype(F32)).astype(BF)


def head_mask(inner):
    heads = lax.broadcasted_iota(jnp.int32, (HEADS, inner), 0)
    owner = lax.broadcasted_iota(jnp.int32, (HEADS, inner), 1) // HEAD_DIM
    return heads == owner


def by_head(query, mask):
    spread_out = jnp.where(mask[None], query[:, None, :], jnp.zeros((), BF))
    return spread_out.reshape(STEPS * HEADS, -1)


def own_heads(mixed, mask):
    inner = mask.shape[1]
    kept = jnp.where(mask[None], mixed.reshape(STEPS, HEADS, inner), 0.0)
    return jnp.sum(kept, axis=1).astype(BF)


def attend_self(query, cache_k, cache_v, fresh_k, fresh_v):
    mask = head_mask(query.shape[1])
    wide = by_head(query, mask)
    prefix = cache_k.shape[0]
    step_of = lax.broadcasted_iota(jnp.int32, (STEPS, HEADS, STEPS), 0).reshape(-1, STEPS)
    key_of = lax.broadcasted_iota(jnp.int32, (STEPS * HEADS, STEPS), 1)
    scores_new = jnp.where(key_of <= step_of, 0.125 * dot_t(wide, fresh_k), -jnp.inf)
    scores = jnp.concatenate([0.125 * dot_t(wide, cache_k), scores_new], axis=1)
    weights = jax.nn.softmax(scores, axis=-1).astype(BF)
    mixed = dot(weights[:, :prefix], cache_v) + dot(weights[:, prefix:], fresh_v)
    return own_heads(mixed, mask)


def attend_cross(query, keys, values, length):
    mask = head_mask(query.shape[1])
    scores = 0.125 * dot_t(by_head(query, mask), keys)
    valid = lax.broadcasted_iota(jnp.int32, scores.shape, 1) < length
    weights = jax.nn.softmax(jnp.where(valid, scores, -1e30), axis=-1).astype(BF)
    return own_heads(dot(weights, values), mask)


def to_plane(attended):
    quarters = attended.reshape(STEPS, Z, -1).transpose(1, 0, 2)
    pieces = jnp.broadcast_to(quarters[:, None], (Z, XC) + quarters.shape[1:])
    got = swap(pieces.reshape((PLANE,) + quarters.shape[1:]), ("z", "x", "c"))
    return got.reshape(ROWS, -1)


VMEM = pl.BlockSpec(memory_space=pltpu.VMEM)
SMEM = pl.BlockSpec(memory_space=pltpu.SMEM)


def call(kernel, out_shape, *operands, scalars=0, scratch=(), limit=24):
    return pl.pallas_call(
        kernel,
        out_shape=out_shape,
        in_specs=[SMEM] * scalars + [VMEM] * (len(operands) - scalars),
        out_specs=jax.tree.map(lambda _: VMEM, out_shape),
        scratch_shapes=list(scratch),
        compiler_params=pltpu.CompilerParams(vmem_limit_bytes=limit * 2**20),
    )(*operands)


def table_kernel(place, table, gain, weight, out):
    features = table.shape[0]
    total = jnp.zeros((1, table.shape[1]), F32)
    for i in range(features // 584):
        piece = table[pl.ds(i * 584, 584), :].astype(F32)
        total = total + jnp.sum(piece * piece, axis=0, keepdims=True)
    scale = lax.rsqrt(total / features + 1e-06)
    quarter = weight.shape[1]
    own = table[pl.ds(pl.multiple_of(place[0] * quarter, 16), quarter), :]
    for i in range(3):
        scaled = (weight[i].astype(F32) * gain[...]).astype(BF)
        part = lax.dot_general(scaled, own, (((0,), (0,)), ((), ())), preferred_element_type=F32)
        out[pl.ds(i * 128, 128), :] = (part * scale).astype(BF)


def blocks_kernel(rows, weights, out):
    for i in range(Y):
        out[i] = dot_t(rows[...], weights[i]).astype(BF)


def joined_blocks_kernel(pieces, weights, out):
    rows = jnp.concatenate([pieces[i] for i in range(XC)], axis=1)
    for i in range(Y):
        out[i] = dot_t(rows, weights[i]).astype(BF)


def squares_tail(rows, lanes):
    total = jnp.sum(rows * rows, axis=1, keepdims=True)
    high, low = two_halves(total)
    lane = lax.broadcasted_iota(jnp.int32, (rows.shape[0], lanes), 1)
    first = jnp.where(lane == 0, high.astype(F32), 0.0)
    return jnp.where(lane == 1, low.astype(F32), first)


def cross_query_kernel(pieces, gain, weights, out):
    rows = jnp.concatenate([pieces[i].astype(F32) for i in range(XC)], axis=1)
    out[:, Y * 128 :] = squares_tail(rows, 128).astype(BF)
    rows = (rows * gain[...]).astype(BF)
    for i in range(Y):
        out[:, i * 128 : (i + 1) * 128] = dot(rows, weights[i]).astype(BF)


def gate_up_kernel(place, near, far, gain, weights, out0, out1, out2, out3, rows, result):
    mine = place[1]
    hidden = weights.shape[1]
    for i in range(Y):
        pieces = []
        for j in range(X):
            own, other = near[i * X + j].astype(F32), far[i * X + j].astype(F32)
            pieces += [jnp.where(mine == 0, own, other), jnp.where(mine == 0, other, own)]
        block = jnp.concatenate(pieces, axis=1)
        here = pl.ds(i * ROWS, ROWS)
        result[here, 768:] = squares_tail(block, 128).astype(BF)
        rows[here, :] = (block * gain[...]).astype(BF)
    gate = dot_t(rows[...], weights[0])
    up = dot_t(rows[...], weights[1])
    result[:, :384] = gate[:, :384].astype(BF)
    result[:, 384:768] = up[:, :384].astype(BF)
    lane = lax.broadcasted_iota(jnp.int32, (Y * ROWS, 128), 1)
    last = result[:, 768:].astype(F32)
    for i in range(384, hidden):
        last = jnp.where(lane == i - 384 + 2, gate[:, i : i + 1], last)
        last = jnp.where(lane == i - 384 + 4, up[:, i : i + 1], last)
    result[:, 768:] = last.astype(BF)
    for shift, out in enumerate((out0, out1, out2, out3)):
        start = pl.multiple_of(lax.rem(place[0] + shift, Z) * ROWS, ROWS)
        out[...] = result[pl.ds(start, ROWS), :]


def body(
    token_ids,
    mem_lengths,
    embed_table,
    w_qkv,
    w_self_out,
    w_cross_q,
    w_cross_out,
    w_in,
    w_out,
    lm_head,
    gain_self,
    gain_cross,
    gain_ffn,
    gain_final,
    self_keys,
    self_values,
    cross_keys,
    cross_values,
):
    z, y = lax.axis_index("z"), lax.axis_index("y")
    x, c = lax.axis_index("x"), lax.axis_index("c")
    width = embed_table.shape[1]
    vocab = embed_table.shape[0]
    quarter = width // Z
    block = quarter // XC
    like_state = jax.ShapeDtypeStruct((Y, ROWS, block), BF)

    place = jnp.stack([z, c])

    def part_of(gain):
        return lax.dynamic_slice_in_dim(gain, z * quarter, quarter)[None]

    self_out = lax.all_gather(w_self_out[0].T, "y")
    cross_q = lax.all_gather(w_cross_q[0], "y")
    cross_out = lax.all_gather(w_cross_out[0].T, "y")
    down = lax.all_gather(w_out[0].T, "y")

    digits = jnp.concatenate([token_ids // 16, token_ids % 16], axis=1).astype(BF)
    letters = lm_head.shape[1]
    pieces = lm_head.T.reshape(letters, XC, block).transpose(1, 0, 2)
    pieces = jnp.pad(pieces, ((0, 0), (0, 16 - letters), (0, 256 - block)))
    pieces = pieces.at[:, 15, : 2 * STEPS].set(jnp.broadcast_to(digits, (XC, 2 * STEPS)))
    pieces = jnp.broadcast_to(pieces[None], (Y,) + pieces.shape).reshape(Y * XC, 16, 256)
    got = swap(pieces, ("y", "x", "c"))
    head = got[:, :letters, :block].reshape(-1, block)
    digits = got[:, 15, : 2 * STEPS].astype(jnp.int32)
    tokens = digits[:, :STEPS] * 16 + digits[:, STEPS:]
    tokens = spread(tokens, Z, "z").reshape(Z, Y, XC, STEPS)
    vocab_range = jnp.arange(vocab, dtype=jnp.int32)
    pick_all = (tokens.reshape(-1)[:, None] == vocab_range[None, :]).astype(BF)
    plane_tokens = lax.dynamic_index_in_dim(tokens, y, 1, keepdims=False).reshape(-1)
    pick_plane = (plane_tokens[:, None] == vocab_range[None, :]).astype(BF)
    start = z * quarter + (x * C + c) * block
    state = dot(pick_plane, lax.dynamic_slice_in_dim(embed_table, start, block, axis=1))

    gain = jnp.broadcast_to(part_of(gain_self[0]).T, (quarter, 128))
    table = call(
        table_kernel,
        jax.ShapeDtypeStruct((3 * 128, vocab), BF),
        place,
        embed_table.T,
        gain,
        w_qkv[0].transpose(1, 0, 2),
        scalars=1,
    )
    triple = dot_t(pick_all, table).astype(BF)
    triple = swap(triple.reshape(Z, ROWS, -1), "z").astype(F32).sum(axis=0).astype(BF)
    triple = swap(triple.reshape(Y * XC, STEPS, -1), ("y", "x", "c"))
    triple = triple.reshape(Y * XC, STEPS, 3, -1).transpose(2, 1, 0, 3).reshape(3, STEPS, -1)
    attended = attend_self(triple[0], self_keys[0, 0], self_values[0, 0], triple[1], triple[2])

    parts = swap(call(blocks_kernel, like_state, to_plane(attended), self_out), "z")
    state = state + parts.astype(F32).sum(axis=0).astype(BF).astype(F32)

    parts = call(
        cross_query_kernel,
        jax.ShapeDtypeStruct((ROWS, (Y + 1) * 128), BF),
        spread(state.astype(BF), XC, ("x", "c")),
        part_of(gain_cross[0]),
        cross_q,
    )
    parts = swap(parts.reshape(PLANE, STEPS, -1), ("z", "x", "c"))
    parts = parts.astype(F32).reshape(Z, XC, STEPS, -1).sum(axis=0)
    inner = parts.shape[2] - 128
    scale = lax.rsqrt((parts[0, :, inner] + parts[0, :, inner + 1]) / width + 1e-06)
    query = (parts[:, :, :inner] * scale[None, :, None]).astype(BF)
    query = query.reshape(XC, STEPS, Y, -1).transpose(1, 2, 0, 3).reshape(STEPS, -1)
    attended = attend_cross(query, cross_keys[0, 0], cross_values[0, 0], mem_lengths[0])

    parts = swap(call(blocks_kernel, like_state, to_plane(attended), cross_out), "z")
    state = state + parts.astype(F32).sum(axis=0).astype(BF).astype(F32)

    near = spread(state.astype(BF), Y * X, ("y", "x"))
    far = lax.ppermute(near, "c", [(0, 1), (1, 0)])
    weights = w_in[0].transpose(1, 2, 0)
    hidden = weights.shape[1]
    pieces = call(
        gate_up_kernel,
        [jax.ShapeDtypeStruct((ROWS, 896), BF)] * 4,
        place,
        near,
        far,
        part_of(gain_ffn[0]),
        weights,
        scalars=1,
        scratch=(pltpu.VMEM((Z * ROWS, quarter), BF), pltpu.VMEM((Z * ROWS, 896), BF)),
    )
    parts = jnp.zeros((), F32)
    for shift in range(Z):
        pairs = [(i * Y + j, j * Y + (i + shift) % Z) for i in range(Z) for j in range(Y)]
        parts = parts + lax.ppermute(pieces[shift], ("z", "y"), pairs).astype(F32)
    scale = lax.rsqrt((parts[:, 768] + parts[:, 769]) / width + 1e-06)[:, None]
    parts = (parts * scale).astype(BF).astype(F32)
    extra = hidden - 384
    gate = jnp.concatenate([parts[:, :384], parts[:, 770 : 770 + extra]], axis=1)
    up = jnp.concatenate([parts[:, 384:768], parts[:, 772 : 772 + extra]], axis=1)
    hidden = (jax.nn.gelu(gate, approximate=True) * up).astype(BF)

    parts = call(joined_blocks_kernel, like_state, spread(hidden, XC, ("x", "c")), down)
    parts = swap(parts, "z")
    state = state + parts.astype(F32).sum(axis=0).astype(BF).astype(F32)

    squares = two_halves(jnp.sum(state * state, axis=1, keepdims=True))
    rows = (state * lax.dynamic_slice_in_dim(gain_final, start, block)[None]).astype(BF)
    tail = jnp.concatenate(squares + (jnp.zeros((ROWS, 126), BF),), axis=1)
    parts = jnp.concatenate([dot_t(rows, head).astype(BF), tail], axis=1)
    parts = swap(parts.reshape(PLANE, STEPS, -1), ("z", "x", "c")).astype(F32).sum(axis=0)
    scale = lax.rsqrt((parts[:, vocab] + parts[:, vocab + 1]) / width + 1e-06)
    return (parts[:, :vocab] * scale[:, None]).astype(BF)[:, None, :]


def solution(mesh):
    fine = Mesh(mesh.devices.reshape(Z, Y, X, C), ("z", "y", "x", "c"))
    lines = ("z", "y", "x", "c")
    columns = ("y", "x", "c")
    placed = (
        P(lines, None),
        P(lines),
        P(),
        P(None, "z", None, columns),
        P(None, "z", columns),
        P(None, "z", columns),
        P(None, "z", columns),
        P(None, "z", None, columns),
        P(None, "z", columns),
        P("z", columns),
        P(),
        P(),
        P(),
        P(),
        P(None, lines, None, None),
        P(None, lines, None, None),
        P(None, lines, None, None),
        P(None, lines, None, None),
    )
    return jax.shard_map(
        body, mesh=fine, in_specs=placed, out_specs=P(None, lines, None), check_vma=False
    )
```

```python
import jax
import jax.numpy as jnp
from jax import lax
from jax.experimental import pallas as pl
from jax.experimental.pallas import tpu as pltpu
from jax.sharding import Mesh, PartitionSpec as P

HEADS = 64
HEAD_DIM = 64
STEPS = 3
Z, Y, X, C = 4, 4, 4, 2
XC = X * C
PLANE = Z * XC
ROWS = PLANE * STEPS
GROUPS = ROWS // 16
PACKED = ROWS + 16
BF = jnp.bfloat16
F32 = jnp.float32
VMEM = pl.BlockSpec(memory_space=pltpu.VMEM)
SMEM = pl.BlockSpec(memory_space=pltpu.SMEM)


def swap(pieces, axes):
    return lax.all_to_all(pieces, axes, 0, 0, tiled=True)


def spread(block, count, axes):
    return swap(jnp.broadcast_to(block[None], (count,) + block.shape), axes)


def across(value):
    return lax.ppermute(value, "c", [(0, 1), (1, 0)])


def dot(a, b):
    return jnp.dot(a, b, preferred_element_type=F32)


def dot_t(a, b):
    return lax.dot_general(a, b, (((1,), (1,)), ((), ())), preferred_element_type=F32)


def two_halves(value):
    high = value.astype(BF)
    return high, (value - high.astype(F32)).astype(BF)


def call(kernel, out_shape, *operands, scalars=0, scratch=(), limit=24):
    return pl.pallas_call(
        kernel,
        out_shape=out_shape,
        in_specs=[SMEM] * scalars + [VMEM] * (len(operands) - scalars),
        out_specs=jax.tree.map(lambda _: VMEM, out_shape),
        scratch_shapes=list(scratch),
        compiler_params=pltpu.CompilerParams(vmem_limit_bytes=limit * 2**20),
        cost_estimate=pl.CostEstimate(flops=10**9, bytes_accessed=8 * 10**6, transcendentals=0),
    )(*operands)


def like(*shape, dtype=BF):
    return jax.ShapeDtypeStruct(shape, dtype)


def pack(rows):
    base = rows.shape[1] // 128 * 128
    tail = [rows[i * 16 : (i + 1) * 16, base:] for i in range(GROUPS)]
    empty = base - GROUPS * (rows.shape[1] - base)
    tail.append(jnp.zeros((16, empty), rows.dtype))
    return jnp.concatenate([rows[:, :base], jnp.concatenate(tail, axis=1)], axis=0)


def unpack(packed, width):
    over = width - packed.shape[1]
    tail = [packed[ROWS:, i * over : (i + 1) * over] for i in range(GROUPS)]
    return jnp.concatenate([packed[:ROWS], jnp.concatenate(tail, axis=0)], axis=1)


def by_line(rows, out):
    for i in range(out.shape[0]):
        out[i] = rows[i * STEPS : (i + 1) * STEPS].astype(out.dtype)


def line_rows(got):
    rows = [got[i].astype(F32) for i in range(got.shape[0])]
    return jnp.concatenate(rows, axis=0).astype(BF)


def summed(got, count):
    totals = []
    for i in range(count):
        part = got[i].astype(F32)
        for j in range(1, Z):
            part = part + got[j * count + i].astype(F32)
        totals.append(part)
    return totals


def head_mask(inner):
    heads = lax.broadcasted_iota(jnp.int32, (HEADS, inner), 0)
    owner = lax.broadcasted_iota(jnp.int32, (HEADS, inner), 1) // HEAD_DIM
    return heads == owner


def by_head(query, mask):
    rows = [jnp.where(mask, query[i : i + 1], 0.0).astype(BF) for i in range(STEPS)]
    return jnp.concatenate(rows, axis=0)


def store_attended(mixed, mask, out):
    rows = []
    for i in range(STEPS):
        kept = jnp.where(mask, mixed[i * HEADS : (i + 1) * HEADS], 0.0)
        rows.append(jnp.sum(kept, axis=0, keepdims=True))
    attended = jnp.concatenate(rows, axis=0).astype(BF)
    part = out.shape[2]
    for i in range(PLANE):
        j = i // XC
        out[i] = attended[:, j * part : (j + 1) * part]


def self_kernel(place, got, keys, values, out):
    mine = place[1]
    triple = [[], [], []]
    for total in summed(got, Y * X):
        total = total.astype(BF).astype(F32)
        half = total.shape[1] // C
        for part in by_core(mine, total[:, :half], total[:, half:]):
            for i in range(3):
                triple[i].append(part[:, i * 128 : (i + 1) * 128])
    query, fresh_k, fresh_v = [jnp.concatenate(parts, axis=1) for parts in triple]
    inner = query.shape[1]
    empty = jnp.zeros((8 - STEPS, inner), F32)
    fresh_k = jnp.concatenate([fresh_k, empty], axis=0).astype(BF)
    fresh_v = jnp.concatenate([fresh_v, empty], axis=0).astype(BF)
    mask = head_mask(inner)
    wide = by_head(query, mask)
    step_of = lax.broadcasted_iota(jnp.int32, (STEPS * HEADS, 8), 0) // HEADS
    key_of = lax.broadcasted_iota(jnp.int32, (STEPS * HEADS, 8), 1)
    old = 0.125 * dot_t(wide, keys[...])
    new = jnp.where(key_of <= step_of, 0.125 * dot_t(wide, fresh_k), -jnp.inf)
    top = jnp.maximum(jnp.max(old, axis=1, keepdims=True), jnp.max(new, axis=1, keepdims=True))
    old, new = jnp.exp(old - top), jnp.exp(new - top)
    total = jnp.sum(old, axis=1, keepdims=True) + jnp.sum(new, axis=1, keepdims=True)
    mixed = dot((old / total).astype(BF), values[...]) + dot((new / total).astype(BF), fresh_v)
    store_attended(mixed, mask, out)


def cross_kernel(features, length, got, keys, values, out):
    totals = summed(got, XC)
    inner = Y * 128
    squares = totals[0][:, inner : inner + 1] + totals[0][:, inner + 1 : inner + 2]
    scale = lax.rsqrt(squares / features + 1e-06)
    parts = [total[:, i * 128 : (i + 1) * 128] for i in range(Y) for total in totals]
    query = (jnp.concatenate(parts, axis=1) * scale).astype(BF).astype(F32)
    mask = head_mask(query.shape[1])
    scores = 0.125 * dot_t(by_head(query, mask), keys[...])
    valid = lax.broadcasted_iota(jnp.int32, scores.shape, 1) < length[0]
    scores = jnp.where(valid, scores, -1e30)
    scores = jnp.exp(scores - jnp.max(scores, axis=1, keepdims=True))
    weights = (scores / jnp.sum(scores, axis=1, keepdims=True)).astype(BF)
    store_attended(dot(weights, values[...]), mask, out)


def to_plane(pieces, *early):
    pieces, *early = lax.optimization_barrier((pieces, *early))
    return swap(pieces, ("z", "x", "c")), *early


def pick_kernel(picked, table, other, out):
    rows = jnp.concatenate([dot_t(picked[...], table[...]), other[...].astype(F32)], axis=1)
    by_line(rows, out)


def head_kernel(letters, out):
    count, width = letters.shape
    main = out.shape[1]
    rows = letters[...].astype(F32)
    tail = []
    for i in range(count // 3):
        pieces = [rows[3 * i + j : 3 * i + j + 1, main:] for j in range(3)]
        pieces.append(jnp.zeros((1, main - 3 * (width - main)), F32))
        tail.append(jnp.concatenate(pieces, axis=1))
    out[...] = jnp.concatenate([rows[:, :main]] + tail, axis=0).astype(BF)


def copy_kernel(source, out):
    out[...] = source[...]


def table_kernel(place, table, gain, weight, out):
    features = table.shape[0]
    total = jnp.zeros((1, table.shape[1]), F32)
    for i in range(features // 584):
        piece = table[pl.ds(i * 584, 584), :].astype(F32)
        total = total + jnp.sum(piece * piece, axis=0, keepdims=True)
    scale = lax.rsqrt(total / features + 1e-06)
    quarter = weight.shape[1]
    own = table[pl.ds(pl.multiple_of(place[0] * quarter, 16), quarter), :]
    for i in range(3):
        scaled = (weight[i].astype(F32) * gain[...]).astype(BF)
        part = lax.dot_general(scaled, own, (((0,), (0,)), ((), ())), preferred_element_type=F32)
        out[pl.ds(i * 128, 128), :] = (part * scale).astype(BF)


def blocks_kernel(first, got, weights, out):
    rows = line_rows(got)
    for i in range(Y):
        out[i] = pack(dot_t(rows, weights[i, :, first : first + rows.shape[1]])).astype(BF)


def add_kernel(parts, state, new_state, pieces):
    total = parts[0].astype(F32) + parts[1].astype(F32) + parts[2].astype(F32) + parts[3].astype(F32)
    total = total.astype(BF).astype(F32)
    new = state[...] + unpack(total, state.shape[1])
    new_state[...] = new
    packed = pack(new).astype(BF)
    for i in range(pieces.shape[0]):
        pieces[i] = packed


def squares_tail(rows, lanes):
    total = jnp.sum(rows * rows, axis=1, keepdims=True)
    high, low = two_halves(total)
    lane = lax.broadcasted_iota(jnp.int32, (rows.shape[0], lanes), 1)
    first = jnp.where(lane == 0, high.astype(F32), 0.0)
    return jnp.where(lane == 1, low.astype(F32), first)


def cross_query_kernel(place, pieces, gain, weights, out):
    width = gain.shape[1] // XC
    rows = jnp.concatenate([unpack(pieces[i].astype(F32), width) for i in range(XC)], axis=1)
    tail = squares_tail(rows, 128)
    rows = (rows * gain[pl.ds(place[0], 1), :]).astype(BF)
    parts = []
    for i in range(Y):
        parts.append(dot(rows, weights[i]))
    by_line(jnp.concatenate(parts + [tail], axis=1), out)


def by_core(mine, near, far):
    own, other = near.astype(F32), far.astype(F32)
    return [jnp.where(mine == 0, own, other), jnp.where(mine == 0, other, own)]


def gate_up_kernel(
    place, near, far, gain, weights, out0, out1, out2, out3, rows, result
):
    hidden = weights.shape[1]
    width = gain.shape[1] // XC
    for i in range(Y):
        pieces = []
        for j in range(X):
            pieces += by_core(place[1], near[i * X + j], far[i * X + j])
        block = jnp.concatenate([unpack(piece, width) for piece in pieces], axis=1)
        here = pl.ds(i * ROWS, ROWS)
        result[here, 768:] = squares_tail(block, 128).astype(BF)
        rows[here, :] = (block * gain[pl.ds(place[0], 1), :]).astype(BF)
    gate = dot_t(rows[...], weights[0])
    up = dot_t(rows[...], weights[1])
    result[:, :384] = gate[:, :384].astype(BF)
    result[:, 384:768] = up[:, :384].astype(BF)
    lane = lax.broadcasted_iota(jnp.int32, (Y * ROWS, 128), 1)
    last = result[:, 768:].astype(F32)
    for i in range(384, hidden):
        last = jnp.where(lane == i - 384 + 2, gate[:, i : i + 1], last)
        last = jnp.where(lane == i - 384 + 4, up[:, i : i + 1], last)
    result[:, 768:] = last.astype(BF)
    for shift, out in enumerate((out0, out1, out2, out3)):
        start = pl.multiple_of(lax.rem(place[0] + shift, Z) * ROWS, ROWS)
        out[...] = result[pl.ds(start, ROWS), :]


def hidden_kernel(features, part0, part1, part2, part3, out):
    parts = part0[...].astype(F32) + part1[...].astype(F32)
    parts = parts + part2[...].astype(F32) + part3[...].astype(F32)
    scale = lax.rsqrt((parts[:, 768:769] + parts[:, 769:770]) / features + 1e-06)
    parts = (parts * scale).astype(BF).astype(F32)
    gate = jnp.concatenate([parts[:, :384], parts[:, 770:772]], axis=1)
    up = jnp.concatenate([parts[:, 384:768], parts[:, 772:774]], axis=1)
    packed = pack(jax.nn.gelu(gate, approximate=True) * up).astype(BF)
    for i in range(X):
        out[i] = packed


def down_kernel(place, near, far, weights, state, out):
    pieces = []
    for j in range(X):
        pieces += by_core(place[1], near[j], far[j])
    width = weights.shape[2] // XC
    rows = jnp.concatenate([unpack(piece, width) for piece in pieces], axis=1).astype(BF)
    parts = []
    for i in range(Y):
        part = dot_t(rows, weights[i])
        parts.append(part + jnp.where(place[0] == i, state[...], 0.0))
    parts.append(jnp.zeros((ROWS, out.shape[2] - Y * state.shape[1]), F32))
    by_line(jnp.concatenate(parts, axis=1), out)


def logits_kernel(got, gain, head, out):
    width = gain.shape[1]
    block = width // XC
    total = summed(got, XC)
    main = head.shape[2]
    over = width - main
    squares = jnp.zeros((STEPS, 1), F32)
    sums = jnp.zeros((4 * STEPS, head.shape[1]), F32)
    for i in range(Y):
        rows = jnp.concatenate([part[:, i * block : (i + 1) * block] for part in total], axis=1)
        squares = squares + jnp.sum(rows * rows, axis=1, keepdims=True)
        rows = rows * gain[i : i + 1, :]
        stack = [rows[:, :main]]
        for j in range(3):
            pieces = [rows[:, main:], jnp.zeros((STEPS, main - (j + 1) * over), F32)]
            if j:
                pieces = [jnp.zeros((STEPS, j * over), F32)] + pieces
            stack.append(jnp.concatenate(pieces, axis=1))
        sums = sums + dot_t(jnp.concatenate(stack, axis=0).astype(BF), head[i])
    letters = out.shape[1] // (Y * XC)
    source = lax.broadcasted_iota(jnp.int32, (head.shape[1], out.shape[1]), 0)
    target = lax.broadcasted_iota(jnp.int32, (head.shape[1], out.shape[1]), 1)
    group, letter = target // letters * (letters * 4 // 3), target % letters
    logits = jnp.zeros((STEPS, out.shape[1]), F32)
    for i in range(4):
        if i == 0:
            keep = source == group + letter
        else:
            keep = (source == group + letters + letter // 3) & (letter % 3 == i - 1)
        keep = keep.astype(F32).astype(BF)
        high, low = two_halves(sums[i * STEPS : (i + 1) * STEPS])
        logits = logits + dot(high, keep) + dot(low, keep)
    scale = lax.rsqrt(squares / (width * Y) + 1e-06)
    out[...] = (logits * scale).astype(BF)


def staged(weights):
    return call(copy_kernel, like(*weights.shape), weights)


def body(
    token_ids,
    mem_lengths,
    embed_table,
    w_qkv,
    w_self_out,
    w_cross_q,
    w_cross_out,
    w_in,
    w_out,
    lm_head,
    gain_self,
    gain_cross,
    gain_ffn,
    gain_final,
    self_keys,
    self_values,
    cross_keys,
    cross_values,
):
    z, y = lax.axis_index("z"), lax.axis_index("y")
    x, c = lax.axis_index("x"), lax.axis_index("c")
    vocab, width = embed_table.shape
    quarter = width // Z
    block = quarter // XC
    letters = lm_head.shape[1]
    place = jnp.stack([z, c])
    lines = ("z", "y", "x", "c")

    inner = self_keys.shape[3]
    joined = jnp.concatenate([w_self_out[0].T, w_cross_out[0].T], axis=1)
    joined = lax.all_gather(joined, "y")
    cross_q = lax.all_gather(w_cross_q[0], "y")
    down = lax.all_gather(w_out[0].T, "y")
    head = lax.all_gather(call(head_kernel, like(letters * 4 // 3, 896), lm_head.T), lines)
    head = head.reshape(Z, -1, 896)

    sibling = across(token_ids)
    pair = jnp.where(c == 0, jnp.stack([token_ids, sibling]), jnp.stack([sibling, token_ids]))
    tokens = spread(pair.reshape(C, STEPS), Z * Y * X, ("z", "y", "x"))
    tokens = tokens.reshape(Z * Y * X, C, STEPS)
    vocab_range = jnp.arange(vocab, dtype=jnp.int32)

    def one_hot(chosen):
        return (chosen.reshape(-1)[:, None] == vocab_range[None, :]).astype(BF)

    plane_tokens = lax.dynamic_index_in_dim(tokens.reshape(Z, Y, XC, STEPS), y, 1, keepdims=False)
    start = z * quarter + (x * C + c) * block
    own_block = lax.dynamic_slice_in_dim(embed_table, start, block, axis=1)
    state = dot(one_hot(plane_tokens), own_block)

    gain = lax.dynamic_slice_in_dim(gain_self[0], z * quarter, quarter)
    table = call(
        table_kernel,
        like(3 * 128, vocab),
        place,
        embed_table.T,
        jnp.broadcast_to(gain[:, None], (quarter, 128)),
        w_qkv[0].transpose(1, 0, 2),
        scalars=1,
    )
    mine = lax.dynamic_index_in_dim(tokens, c, 1, keepdims=False)
    theirs = lax.dynamic_index_in_dim(tokens, 1 - c, 1, keepdims=False)
    other = across(dot_t(one_hot(theirs), table).astype(BF))
    pieces = call(
        pick_kernel, like(Z * Y * X, STEPS, C * 384), one_hot(mine), table, other
    )
    got = swap(pieces, ("z", "y", "x"))
    for_plane = like(PLANE, STEPS, inner // Z)
    pieces = call(
        self_kernel, for_plane, place, got, self_keys[0, 0], self_values[0, 0], scalars=1
    )

    got, joined, w_in = to_plane(pieces, joined, w_in)
    weights = w_in[0].transpose(1, 2, 0)

    joined = staged(joined)

    def blocks(got, first):
        return call(
            lambda *refs: blocks_kernel(first, *refs), like(Y, PACKED, 128), got, joined
        )

    parts = swap(blocks(got, 0), "z")
    state, pieces = call(
        add_kernel, (like(ROWS, block, dtype=F32), like(XC, PACKED, 128)), parts, state
    )

    gain = gain_cross[0].reshape(Z, quarter)
    pieces, cross_q = lax.optimization_barrier((pieces, cross_q))
    pieces = swap(pieces, ("x", "c"))
    cross_q = staged(cross_q)
    parts = call(
        cross_query_kernel,
        like(PLANE, STEPS, (Y + 1) * 128),
        place,
        pieces,
        gain,
        cross_q,
        scalars=1,
    )
    parts, cross_values = lax.optimization_barrier((parts, cross_values))
    got = swap(parts, ("z", "x", "c"))
    pieces = call(
        lambda *refs: cross_kernel(width, *refs),
        for_plane,
        mem_lengths,
        got,
        cross_keys[0, 0],
        staged(cross_values[0, 0]),
        scalars=1,
    )

    got, = to_plane(pieces)
    parts = swap(blocks(got, inner // Z), "z")
    state, pieces = call(
        add_kernel, (like(ROWS, block, dtype=F32), like(Y * X, PACKED, 128)), parts, state
    )

    gain = gain_ffn[0].reshape(Z, quarter)
    pieces, down = lax.optimization_barrier((pieces, down))
    near = swap(pieces, ("y", "x"))
    down = staged(down)
    pieces = call(
        gate_up_kernel,
        [like(ROWS, 896)] * 4,
        place,
        near,
        across(near),
        gain,
        weights,
        scalars=1,
        scratch=(pltpu.VMEM((Z * ROWS, quarter), BF), pltpu.VMEM((Z * ROWS, 896), BF)),
    )
    parts = []
    for shift in range(Z):
        pairs = [(i * Y + j, j * Y + (i + shift) % Z) for i in range(Z) for j in range(Y)]
        parts.append(lax.ppermute(pieces[shift], ("z", "y"), pairs))
    pieces = call(lambda *refs: hidden_kernel(width, *refs), like(X, PACKED, 384), *parts)

    near = swap(pieces, "x")
    parts = call(
        down_kernel,
        like(PLANE, STEPS, 640),
        place,
        near,
        across(near),
        down,
        state,
        scalars=1,
    )
    gain = gain_final.reshape(Z, quarter)
    got = swap(parts, ("z", "x", "c"))
    return call(logits_kernel, like(STEPS, vocab), got, gain, head)[:, None, :]


def solution(mesh):
    fine = Mesh(mesh.devices.reshape(Z, Y, X, C), ("z", "y", "x", "c"))
    lines = ("z", "y", "x", "c")
    columns = ("y", "x", "c")
    placed = (
        P(lines, None),
        P(lines),
        P(),
        P(None, "z", None, columns),
        P(None, "z", columns),
        P(None, "z", columns),
        P(None, "z", columns),
        P(None, "z", None, columns),
        P(None, "z", columns),
        P("z", columns),
        P(),
        P(),
        P(),
        P(),
        P(None, lines, None, None),
        P(None, lines, None, None),
        P(None, lines, None, None),
        P(None, lines, None, None),
    )
    return jax.shard_map(
        body, mesh=fine, in_specs=placed, out_specs=P(None, lines, None), check_vma=False
    )
```

```python
import jax
import jax.numpy as jnp
from jax import lax
from jax.experimental import pallas as pl
from jax.experimental.pallas import tpu as pltpu
from jax.sharding import Mesh, PartitionSpec as P

HEADS = 64
HEAD_DIM = 64
STEPS = 3
Z, Y, X, C = 4, 4, 4, 2
XC = X * C
PLANE = Z * XC
ROWS = PLANE * STEPS
GROUPS = ROWS // 16
PACKED = ROWS + 16
BF = jnp.bfloat16
F32 = jnp.float32
VMEM = pl.BlockSpec(memory_space=pltpu.VMEM)
SMEM = pl.BlockSpec(memory_space=pltpu.SMEM)


def swap(pieces, axes):
    return lax.all_to_all(pieces, axes, 0, 0, tiled=True)


def spread(block, count, axes):
    return swap(jnp.broadcast_to(block[None], (count,) + block.shape), axes)


def across(value):
    return lax.ppermute(value, "c", [(0, 1), (1, 0)])


def dot(a, b):
    return jnp.dot(a, b, preferred_element_type=F32)


def dot_t(a, b):
    return lax.dot_general(a, b, (((1,), (1,)), ((), ())), preferred_element_type=F32)


def two_halves(value):
    high = value.astype(BF)
    return high, (value - high.astype(F32)).astype(BF)


def call(kernel, out_shape, *operands, scalars=0, scratch=(), limit=24):
    return pl.pallas_call(
        kernel,
        out_shape=out_shape,
        in_specs=[SMEM] * scalars + [VMEM] * (len(operands) - scalars),
        out_specs=jax.tree.map(lambda _: VMEM, out_shape),
        scratch_shapes=list(scratch),
        compiler_params=pltpu.CompilerParams(vmem_limit_bytes=limit * 2**20),
        cost_estimate=pl.CostEstimate(flops=10**9, bytes_accessed=8 * 10**6, transcendentals=0),
    )(*operands)


def like(*shape, dtype=BF):
    return jax.ShapeDtypeStruct(shape, dtype)


def pack(rows):
    base = rows.shape[1] // 128 * 128
    tail = [rows[i * 16 : (i + 1) * 16, base:] for i in range(GROUPS)]
    empty = base - GROUPS * (rows.shape[1] - base)
    tail.append(jnp.zeros((16, empty), rows.dtype))
    return jnp.concatenate([rows[:, :base], jnp.concatenate(tail, axis=1)], axis=0)


def unpack(packed, width):
    over = width - packed.shape[1]
    tail = [packed[ROWS:, i * over : (i + 1) * over] for i in range(GROUPS)]
    return jnp.concatenate([packed[:ROWS], jnp.concatenate(tail, axis=0)], axis=1)


def by_line(rows, out):
    for i in range(out.shape[0]):
        out[i] = rows[i * STEPS : (i + 1) * STEPS].astype(out.dtype)


def line_rows(got):
    rows = [got[i].astype(F32) for i in range(got.shape[0])]
    return jnp.concatenate(rows, axis=0).astype(BF)


def summed(got, count):
    totals = []
    for i in range(count):
        part = got[i].astype(F32)
        for j in range(1, Z):
            part = part + got[j * count + i].astype(F32)
        totals.append(part)
    return totals


def head_mask(inner):
    heads = lax.broadcasted_iota(jnp.int32, (HEADS, inner), 0)
    owner = lax.broadcasted_iota(jnp.int32, (HEADS, inner), 1) // HEAD_DIM
    return heads == owner


def by_head(query, mask):
    rows = [jnp.where(mask, query[i : i + 1], 0.0).astype(BF) for i in range(STEPS)]
    return jnp.concatenate(rows, axis=0)


def store_attended(mixed, mask, out):
    rows = []
    for i in range(STEPS):
        kept = jnp.where(mask, mixed[i * HEADS : (i + 1) * HEADS], 0.0)
        rows.append(jnp.sum(kept, axis=0, keepdims=True))
    attended = jnp.concatenate(rows, axis=0).astype(BF)
    part = out.shape[2]
    for i in range(PLANE):
        j = i // XC
        out[i] = attended[:, j * part : (j + 1) * part]


def self_kernel(got, keys, values, out):
    triple = [[], [], []]
    for total in summed(got, PLANE):
        total = total.astype(BF).astype(F32)
        for i in range(3):
            triple[i].append(total[:, i * 128 : (i + 1) * 128])
    query, fresh_k, fresh_v = [jnp.concatenate(parts, axis=1) for parts in triple]
    inner = query.shape[1]
    empty = jnp.zeros((8 - STEPS, inner), F32)
    fresh_k = jnp.concatenate([fresh_k, empty], axis=0).astype(BF)
    fresh_v = jnp.concatenate([fresh_v, empty], axis=0).astype(BF)
    mask = head_mask(inner)
    wide = by_head(query, mask)
    step_of = lax.broadcasted_iota(jnp.int32, (STEPS * HEADS, 8), 0) // HEADS
    key_of = lax.broadcasted_iota(jnp.int32, (STEPS * HEADS, 8), 1)
    old = 0.125 * dot_t(wide, keys[...])
    new = jnp.where(key_of <= step_of, 0.125 * dot_t(wide, fresh_k), -jnp.inf)
    top = jnp.maximum(jnp.max(old, axis=1, keepdims=True), jnp.max(new, axis=1, keepdims=True))
    old, new = jnp.exp(old - top), jnp.exp(new - top)
    total = jnp.sum(old, axis=1, keepdims=True) + jnp.sum(new, axis=1, keepdims=True)
    mixed = dot((old / total).astype(BF), values[...]) + dot((new / total).astype(BF), fresh_v)
    store_attended(mixed, mask, out)


def cross_kernel(features, length, got, keys0, keys1, values, out):
    totals = summed(got, XC)
    inner = Y * 128
    squares = totals[0][:, inner : inner + 1] + totals[0][:, inner + 1 : inner + 2]
    scale = lax.rsqrt(squares / features + 1e-06)
    parts = [total[:, i * 128 : (i + 1) * 128] for i in range(Y) for total in totals]
    query = (jnp.concatenate(parts, axis=1) * scale).astype(BF).astype(F32)
    mask = head_mask(query.shape[1])
    wide = by_head(query, mask)
    scores = [0.125 * dot_t(wide, keys[...]) for keys in (keys0, keys1)]
    scores = jnp.concatenate(scores, axis=1)
    valid = lax.broadcasted_iota(jnp.int32, scores.shape, 1) < length[0]
    scores = jnp.where(valid, scores, -1e30)
    scores = jnp.exp(scores - jnp.max(scores, axis=1, keepdims=True))
    weights = (scores / jnp.sum(scores, axis=1, keepdims=True)).astype(BF)
    store_attended(dot(weights, values[...]), mask, out)


def to_plane(pieces, *early):
    pieces, *early = lax.optimization_barrier((pieces, *early))
    return swap(pieces, ("z", "x", "c")), *early


def pick_kernel(picked, table, out):
    by_line(dot_t(picked[...], table[...]), out)


def head_kernel(letters, out):
    count, width = letters.shape
    main = out.shape[1]
    rows = letters[...].astype(F32)
    tail = []
    for i in range(count // 3):
        pieces = [rows[3 * i + j : 3 * i + j + 1, main:] for j in range(3)]
        pieces.append(jnp.zeros((1, main - 3 * (width - main)), F32))
        tail.append(jnp.concatenate(pieces, axis=1))
    out[...] = jnp.concatenate([rows[:, :main]] + tail, axis=0).astype(BF)


def turned_blocks_kernel(place, got, own, next1, next2, next3, out):
    rows = line_rows(got)
    for i, weights in enumerate((own, next1, next2, next3)):
        block = pack(dot_t(rows, weights[...])).astype(BF)
        out[pl.ds(lax.rem(place[2] + i, Y), 1)] = block[None]


def copy_kernel(source, out):
    out[...] = source[...]


def table_kernel(place, table, gain, weight, out):
    features = table.shape[0]
    total = jnp.zeros((1, table.shape[1]), F32)
    for i in range(features // 584):
        piece = table[pl.ds(i * 584, 584), :].astype(F32)
        total = total + jnp.sum(piece * piece, axis=0, keepdims=True)
    scale = lax.rsqrt(total / features + 1e-06)
    quarter = weight.shape[1]
    own = table[pl.ds(pl.multiple_of(place[0] * quarter, 16), quarter), :]
    for i in range(3):
        scaled = (weight[i].astype(F32) * gain[...]).astype(BF)
        part = lax.dot_general(scaled, own, (((0,), (0,)), ((), ())), preferred_element_type=F32)
        out[pl.ds(i * 128, 128), :] = (part * scale).astype(BF)


def blocks_kernel(got, weights, out):
    rows = line_rows(got)
    for i in range(Y):
        out[i] = pack(dot_t(rows, weights[i])).astype(BF)


def add_kernel(parts, state, new_state, pieces):
    total = parts[0].astype(F32) + parts[1].astype(F32) + parts[2].astype(F32) + parts[3].astype(F32)
    total = total.astype(BF).astype(F32)
    new = state[...] + unpack(total, state.shape[1])
    new_state[...] = new
    packed = pack(new).astype(BF)
    for i in range(pieces.shape[0]):
        pieces[i] = packed


def squares_tail(rows, lanes):
    total = jnp.sum(rows * rows, axis=1, keepdims=True)
    high, low = two_halves(total)
    lane = lax.broadcasted_iota(jnp.int32, (rows.shape[0], lanes), 1)
    first = jnp.where(lane == 0, high.astype(F32), 0.0)
    return jnp.where(lane == 1, low.astype(F32), first)


def cross_query_kernel(place, pieces, gain, weights, out):
    width = gain.shape[1] // XC
    rows = jnp.concatenate([unpack(pieces[i].astype(F32), width) for i in range(XC)], axis=1)
    tail = squares_tail(rows, 128)
    rows = (rows * gain[pl.ds(place[0], 1), :]).astype(BF)
    parts = []
    for i in range(Y):
        parts.append(dot(rows, weights[i]))
    by_line(jnp.concatenate(parts + [tail], axis=1), out)


def by_core(mine, near, far):
    own, other = near.astype(F32), far.astype(F32)
    return [jnp.where(mine == 0, own, other), jnp.where(mine == 0, other, own)]


def gate_up_kernel(
    place, near, far, gain, weights, out0, out1, out2, out3, rows, result
):
    hidden = weights.shape[1]
    width = gain.shape[1] // XC
    for i in range(Y):
        pieces = []
        for j in range(X):
            pieces += by_core(place[1], near[i * X + j], far[i * X + j])
        block = jnp.concatenate([unpack(piece, width) for piece in pieces], axis=1)
        here = pl.ds(i * ROWS, ROWS)
        result[here, 768:] = squares_tail(block, 128).astype(BF)
        rows[here, :] = (block * gain[pl.ds(place[0], 1), :]).astype(BF)
    gate = dot_t(rows[...], weights[0])
    up = dot_t(rows[...], weights[1])
    result[:, :384] = gate[:, :384].astype(BF)
    result[:, 384:768] = up[:, :384].astype(BF)
    lane = lax.broadcasted_iota(jnp.int32, (Y * ROWS, 128), 1)
    last = result[:, 768:].astype(F32)
    for i in range(384, hidden):
        last = jnp.where(lane == i - 384 + 2, gate[:, i : i + 1], last)
        last = jnp.where(lane == i - 384 + 4, up[:, i : i + 1], last)
    result[:, 768:] = last.astype(BF)
    for shift, out in enumerate((out0, out1, out2, out3)):
        start = pl.multiple_of(lax.rem(place[0] + shift, Z) * ROWS, ROWS)
        out[...] = result[pl.ds(start, ROWS), :]


def hidden_kernel(features, part0, part1, part2, part3, out):
    parts = part0[...].astype(F32) + part1[...].astype(F32)
    parts = parts + part2[...].astype(F32) + part3[...].astype(F32)
    scale = lax.rsqrt((parts[:, 768:769] + parts[:, 769:770]) / features + 1e-06)
    parts = (parts * scale).astype(BF).astype(F32)
    gate = jnp.concatenate([parts[:, :384], parts[:, 770:772]], axis=1)
    up = jnp.concatenate([parts[:, 384:768], parts[:, 772:774]], axis=1)
    packed = pack(jax.nn.gelu(gate, approximate=True) * up).astype(BF)
    for i in range(X):
        out[i] = packed


def down_kernel(place, near, far, weights, state, out):
    pieces = []
    for j in range(X):
        pieces += by_core(place[1], near[j], far[j])
    width = weights.shape[2] // XC
    rows = jnp.concatenate([unpack(piece, width) for piece in pieces], axis=1).astype(BF)
    parts = []
    for i in range(Y):
        part = dot_t(rows, weights[i])
        parts.append(part + jnp.where(place[0] == i, state[...], 0.0))
    parts.append(jnp.zeros((ROWS, out.shape[2] - Y * state.shape[1]), F32))
    by_line(jnp.concatenate(parts, axis=1), out)


def logits_kernel(got, gain, head, out):
    width = gain.shape[1]
    block = width // XC
    total = summed(got, XC)
    main = head.shape[2]
    over = width - main
    squares = jnp.zeros((STEPS, 1), F32)
    sums = jnp.zeros((4 * STEPS, head.shape[1]), F32)
    for i in range(Y):
        rows = jnp.concatenate([part[:, i * block : (i + 1) * block] for part in total], axis=1)
        squares = squares + jnp.sum(rows * rows, axis=1, keepdims=True)
        rows = rows * gain[i : i + 1, :]
        stack = [rows[:, :main]]
        for j in range(3):
            pieces = [rows[:, main:], jnp.zeros((STEPS, main - (j + 1) * over), F32)]
            if j:
                pieces = [jnp.zeros((STEPS, j * over), F32)] + pieces
            stack.append(jnp.concatenate(pieces, axis=1))
        sums = sums + dot_t(jnp.concatenate(stack, axis=0).astype(BF), head[i])
    letters = out.shape[1] // (Y * XC)
    source = lax.broadcasted_iota(jnp.int32, (head.shape[1], out.shape[1]), 0)
    target = lax.broadcasted_iota(jnp.int32, (head.shape[1], out.shape[1]), 1)
    group, letter = target // letters * (letters * 4 // 3), target % letters
    logits = jnp.zeros((STEPS, out.shape[1]), F32)
    for i in range(4):
        if i == 0:
            keep = source == group + letter
        else:
            keep = (source == group + letters + letter // 3) & (letter % 3 == i - 1)
        keep = keep.astype(F32).astype(BF)
        high, low = two_halves(sums[i * STEPS : (i + 1) * STEPS])
        logits = logits + dot(high, keep) + dot(low, keep)
    scale = lax.rsqrt(squares / (width * Y) + 1e-06)
    out[...] = (logits * scale).astype(BF)


def turned(weights):
    parts = [weights]
    for shift in range(1, Y):
        pairs = [(i, (i - shift) % Y) for i in range(Y)]
        parts.append(lax.ppermute(weights, "y", pairs))
    return parts


def staged(weights):
    return call(copy_kernel, like(*weights.shape), weights)


def body(
    token_ids,
    mem_lengths,
    embed_table,
    w_qkv,
    w_self_out,
    w_cross_q,
    w_cross_out,
    w_in,
    w_out,
    lm_head,
    gain_self,
    gain_cross,
    gain_ffn,
    gain_final,
    self_keys,
    self_values,
    cross_keys,
    cross_values,
):
    z, y = lax.axis_index("z"), lax.axis_index("y")
    x, c = lax.axis_index("x"), lax.axis_index("c")
    vocab, width = embed_table.shape
    quarter = width // Z
    block = quarter // XC
    letters = lm_head.shape[1]
    place = jnp.stack([z, c, y])
    lines = ("z", "y", "x", "c")

    inner = self_keys.shape[3]
    self_out = lax.all_gather(w_self_out[0].T, "y")

    sibling = across(token_ids)
    pair = jnp.where(c == 0, jnp.stack([token_ids, sibling]), jnp.stack([sibling, token_ids]))
    tokens = jnp.broadcast_to(pair.reshape(1, C, STEPS), (Z * Y * X, C, STEPS))
    tokens, w_cross_q, w_out, lm_head = lax.optimization_barrier(
        (tokens, w_cross_q, w_out, lm_head)
    )
    cross_q = lax.all_gather(w_cross_q[0], "y")
    down = lax.all_gather(w_out[0].T, "y")
    head = lax.all_gather(call(head_kernel, like(letters * 4 // 3, 896), lm_head.T), lines)
    head = head.reshape(Z, -1, 896)
    tokens = swap(tokens, ("z", "y", "x"))
    tokens = tokens.reshape(Z * Y * X, C, STEPS)
    vocab_range = jnp.arange(vocab, dtype=jnp.int32)

    def one_hot(chosen):
        return (chosen.reshape(-1)[:, None] == vocab_range[None, :]).astype(BF)

    plane_tokens = lax.dynamic_index_in_dim(tokens.reshape(Z, Y, XC, STEPS), y, 1, keepdims=False)
    start = z * quarter + (x * C + c) * block
    own_block = lax.dynamic_slice_in_dim(embed_table, start, block, axis=1)
    state = dot(one_hot(plane_tokens), own_block)

    gain = lax.dynamic_slice_in_dim(gain_self[0], z * quarter, quarter)
    table = call(
        table_kernel,
        like(3 * 128, vocab),
        place,
        embed_table.T,
        jnp.broadcast_to(gain[:, None], (quarter, 128)),
        w_qkv[0].transpose(1, 0, 2),
        scalars=1,
    )
    pieces = call(
        pick_kernel, like(Z * PLANE, STEPS, 3 * 128), one_hot(tokens), table
    )
    got = swap(pieces, ("z", "y", "x", "c"))
    for_plane = like(PLANE, STEPS, inner // Z)
    pieces = call(self_kernel, for_plane, got, self_keys[0, 0], self_values[0, 0])

    got, self_out, w_in, w_cross_out = to_plane(pieces, self_out, w_in, w_cross_out)
    cross_out = turned(w_cross_out[0].T)
    weights = w_in[0].transpose(1, 2, 0)
    parts = swap(call(blocks_kernel, like(Y, PACKED, 128), got, staged(self_out)), "z")
    state, pieces = call(
        add_kernel, (like(ROWS, block, dtype=F32), like(XC, PACKED, 128)), parts, state
    )

    gain = gain_cross[0].reshape(Z, quarter)
    pieces, cross_q, *cross_out = lax.optimization_barrier((pieces, cross_q, *cross_out))
    pieces = swap(pieces, ("x", "c"))
    cross_q = staged(cross_q)
    parts = call(
        cross_query_kernel,
        like(PLANE, STEPS, (Y + 1) * 128),
        place,
        pieces,
        gain,
        cross_q,
        scalars=1,
    )
    parts, cross_values, cross_keys = lax.optimization_barrier(
        (parts, cross_values, cross_keys)
    )
    got = swap(parts, ("z", "x", "c"))
    pieces = call(
        lambda *refs: cross_kernel(width, *refs),
        for_plane,
        mem_lengths,
        got,
        cross_keys[0, 0, :128],
        cross_keys[0, 0, 128:],
        staged(cross_values[0, 0]),
        scalars=1,
    )

    got, = to_plane(pieces)
    parts = call(turned_blocks_kernel, like(Y, PACKED, 128), place, got, *cross_out, scalars=1)
    parts = swap(parts, "z")
    state, pieces = call(
        add_kernel, (like(ROWS, block, dtype=F32), like(Y * X, PACKED, 128)), parts, state
    )

    gain = gain_ffn[0].reshape(Z, quarter)
    pieces, down = lax.optimization_barrier((pieces, down))
    near = swap(pieces, ("y", "x"))
    down = staged(down)
    pieces = call(
        gate_up_kernel,
        [like(ROWS, 896)] * 4,
        place,
        near,
        across(near),
        gain,
        weights,
        scalars=1,
        scratch=(pltpu.VMEM((Z * ROWS, quarter), BF), pltpu.VMEM((Z * ROWS, 896), BF)),
    )
    parts = []
    for shift in range(Z):
        pairs = [(i * Y + j, j * Y + (i + shift) % Z) for i in range(Z) for j in range(Y)]
        parts.append(lax.ppermute(pieces[shift], ("z", "y"), pairs))
    pieces = call(lambda *refs: hidden_kernel(width, *refs), like(X, PACKED, 384), *parts)

    near = swap(pieces, "x")
    parts = call(
        down_kernel,
        like(PLANE, STEPS, 640),
        place,
        near,
        across(near),
        down,
        state,
        scalars=1,
    )
    gain = gain_final.reshape(Z, quarter)
    got = swap(parts, ("z", "x", "c"))
    return call(logits_kernel, like(STEPS, vocab), got, gain, head)[:, None, :]


def solution(mesh):
    fine = Mesh(mesh.devices.reshape(Z, Y, X, C), ("z", "y", "x", "c"))
    lines = ("z", "y", "x", "c")
    columns = ("y", "x", "c")
    placed = (
        P(lines, None),
        P(lines),
        P(),
        P(None, "z", None, columns),
        P(None, "z", columns),
        P(None, "z", columns),
        P(None, "z", columns),
        P(None, "z", None, columns),
        P(None, "z", columns),
        P("z", columns),
        P(),
        P(),
        P(),
        P(),
        P(None, lines, None, None),
        P(None, lines, None, None),
        P(None, lines, None, None),
        P(None, lines, None, None),
    )
    return jax.shard_map(
        body, mesh=fine, in_specs=placed, out_specs=P(None, lines, None), check_vma=False
    )
```

```python
import jax
import jax.numpy as jnp
from jax import lax
from jax.experimental import pallas as pl
from jax.experimental.pallas import tpu as pltpu
from jax.sharding import Mesh, PartitionSpec as P

HEADS = 64
HEAD_DIM = 64
STEPS = 3
Z, Y, X, C = 4, 4, 4, 2
XC = X * C
PLANE = Z * XC
ROWS = PLANE * STEPS
GROUPS = ROWS // 16
PACKED = ROWS + 16
BF = jnp.bfloat16
F32 = jnp.float32
VMEM = pl.BlockSpec(memory_space=pltpu.VMEM)
SMEM = pl.BlockSpec(memory_space=pltpu.SMEM)


def swap(pieces, axes):
    return lax.all_to_all(pieces, axes, 0, 0, tiled=True)


def spread(block, count, axes):
    return swap(jnp.broadcast_to(block[None], (count,) + block.shape), axes)


def across(value):
    return lax.ppermute(value, "c", [(0, 1), (1, 0)])


def dot(a, b):
    return jnp.dot(a, b, preferred_element_type=F32)


def dot_t(a, b):
    return lax.dot_general(a, b, (((1,), (1,)), ((), ())), preferred_element_type=F32)


def two_halves(value):
    high = value.astype(BF)
    return high, (value - high.astype(F32)).astype(BF)


def call(kernel, out_shape, *operands, scalars=0, scratch=(), limit=24):
    return pl.pallas_call(
        kernel,
        out_shape=out_shape,
        in_specs=[SMEM] * scalars + [VMEM] * (len(operands) - scalars),
        out_specs=jax.tree.map(lambda _: VMEM, out_shape),
        scratch_shapes=list(scratch),
        compiler_params=pltpu.CompilerParams(vmem_limit_bytes=limit * 2**20),
        cost_estimate=pl.CostEstimate(flops=10**9, bytes_accessed=8 * 10**6, transcendentals=0),
    )(*operands)


def like(*shape, dtype=BF):
    return jax.ShapeDtypeStruct(shape, dtype)


def pack(rows):
    base = rows.shape[1] // 128 * 128
    tail = [rows[i * 16 : (i + 1) * 16, base:] for i in range(GROUPS)]
    empty = base - GROUPS * (rows.shape[1] - base)
    tail.append(jnp.zeros((16, empty), rows.dtype))
    return jnp.concatenate([rows[:, :base], jnp.concatenate(tail, axis=1)], axis=0)


def unpack(packed, width):
    over = width - packed.shape[1]
    tail = [packed[ROWS:, i * over : (i + 1) * over] for i in range(GROUPS)]
    return jnp.concatenate([packed[:ROWS], jnp.concatenate(tail, axis=0)], axis=1)


def by_line(rows, out):
    for i in range(out.shape[0]):
        out[i] = rows[i * STEPS : (i + 1) * STEPS].astype(out.dtype)


def line_rows(got):
    rows = [got[i].astype(F32) for i in range(got.shape[0])]
    return jnp.concatenate(rows, axis=0).astype(BF)


def summed(got, count):
    totals = []
    for i in range(count):
        part = got[i].astype(F32)
        for j in range(1, Z):
            part = part + got[j * count + i].astype(F32)
        totals.append(part)
    return totals


def head_mask(inner):
    heads = lax.broadcasted_iota(jnp.int32, (HEADS, inner), 0)
    owner = lax.broadcasted_iota(jnp.int32, (HEADS, inner), 1) // HEAD_DIM
    return heads == owner


def by_head(query, mask):
    rows = [jnp.where(mask, query[i : i + 1], 0.0).astype(BF) for i in range(STEPS)]
    return jnp.concatenate(rows, axis=0)


def store_attended(mixed, mask, out):
    rows = []
    for i in range(STEPS):
        kept = jnp.where(mask, mixed[i * HEADS : (i + 1) * HEADS], 0.0)
        rows.append(jnp.sum(kept, axis=0, keepdims=True))
    attended = jnp.concatenate(rows, axis=0).astype(BF)
    part = out.shape[2]
    for i in range(PLANE):
        j = i // XC
        out[i] = attended[:, j * part : (j + 1) * part]


def self_kernel(got, keys, values, out):
    triple = [[], [], []]
    for total in summed(got, PLANE):
        total = total.astype(BF).astype(F32)
        for i in range(3):
            triple[i].append(total[:, i * 128 : (i + 1) * 128])
    query, fresh_k, fresh_v = [jnp.concatenate(parts, axis=1) for parts in triple]
    inner = query.shape[1]
    empty = jnp.zeros((8 - STEPS, inner), F32)
    fresh_k = jnp.concatenate([fresh_k, empty], axis=0).astype(BF)
    fresh_v = jnp.concatenate([fresh_v, empty], axis=0).astype(BF)
    mask = head_mask(inner)
    wide = by_head(query, mask)
    step_of = lax.broadcasted_iota(jnp.int32, (STEPS * HEADS, 8), 0) // HEADS
    key_of = lax.broadcasted_iota(jnp.int32, (STEPS * HEADS, 8), 1)
    old = 0.125 * dot_t(wide, keys[...])
    new = jnp.where(key_of <= step_of, 0.125 * dot_t(wide, fresh_k), -jnp.inf)
    top = jnp.maximum(jnp.max(old, axis=1, keepdims=True), jnp.max(new, axis=1, keepdims=True))
    old, new = jnp.exp(old - top), jnp.exp(new - top)
    total = jnp.sum(old, axis=1, keepdims=True) + jnp.sum(new, axis=1, keepdims=True)
    mixed = dot((old / total).astype(BF), values[...]) + dot((new / total).astype(BF), fresh_v)
    store_attended(mixed, mask, out)


def cross_kernel(features, length, got, keys0, keys1, values, out):
    totals = summed(got, XC)
    inner = Y * 128
    squares = totals[0][:, inner : inner + 1] + totals[0][:, inner + 1 : inner + 2]
    scale = lax.rsqrt(squares / features + 1e-06)
    parts = [total[:, i * 128 : (i + 1) * 128] for i in range(Y) for total in totals]
    query = (jnp.concatenate(parts, axis=1) * scale).astype(BF).astype(F32)
    mask = head_mask(query.shape[1])
    wide = by_head(query, mask)
    scores = [0.125 * dot_t(wide, keys[...]) for keys in (keys0, keys1)]
    scores = jnp.concatenate(scores, axis=1)
    valid = lax.broadcasted_iota(jnp.int32, scores.shape, 1) < length[0]
    scores = jnp.where(valid, scores, -1e30)
    scores = jnp.exp(scores - jnp.max(scores, axis=1, keepdims=True))
    weights = (scores / jnp.sum(scores, axis=1, keepdims=True)).astype(BF)
    store_attended(dot(weights, values[...]), mask, out)


def to_plane(pieces, *early):
    pieces, *early = lax.optimization_barrier((pieces, *early))
    return swap(pieces, ("z", "x", "c")), *early


def pick_kernel(picked, table, out):
    by_line(dot_t(picked[...], table[...]), out)


def head_kernel(letters, out):
    count, width = letters.shape
    main = out.shape[1]
    rows = letters[...].astype(F32)
    tail = []
    for i in range(count // 3):
        pieces = [rows[3 * i + j : 3 * i + j + 1, main:] for j in range(3)]
        pieces.append(jnp.zeros((1, main - 3 * (width - main)), F32))
        tail.append(jnp.concatenate(pieces, axis=1))
    out[...] = jnp.concatenate([rows[:, :main]] + tail, axis=0).astype(BF)


def turned_blocks_kernel(place, got, own, next1, next2, next3, out):
    rows = line_rows(got)
    for i, weights in enumerate((own, next1, next2, next3)):
        block = pack(dot_t(rows, weights[...])).astype(BF)
        out[pl.ds(lax.rem(place[2] + i, Y), 1)] = block[None]


def copy_kernel(source, out):
    out[...] = source[...]


def table_kernel(place, table, gain, weight, out):
    features = table.shape[0]
    total = jnp.zeros((1, table.shape[1]), F32)
    for i in range(features // 584):
        piece = table[pl.ds(i * 584, 584), :].astype(F32)
        total = total + jnp.sum(piece * piece, axis=0, keepdims=True)
    scale = lax.rsqrt(total / features + 1e-06)
    quarter = weight.shape[1]
    own = table[pl.ds(pl.multiple_of(place[0] * quarter, 16), quarter), :]
    for i in range(3):
        scaled = (weight[i].astype(F32) * gain[...]).astype(BF)
        part = lax.dot_general(scaled, own, (((0,), (0,)), ((), ())), preferred_element_type=F32)
        out[pl.ds(i * 128, 128), :] = (part * scale).astype(BF)


def blocks_kernel(got, weights, out):
    rows = line_rows(got)
    for i in range(Y):
        out[i] = pack(dot_t(rows, weights[i])).astype(BF)


def add_kernel(parts, state, new_state, pieces):
    total = parts[0].astype(F32) + parts[1].astype(F32) + parts[2].astype(F32) + parts[3].astype(F32)
    total = total.astype(BF).astype(F32)
    new = state[...] + unpack(total, state.shape[1])
    new_state[...] = new
    packed = pack(new).astype(BF)
    for i in range(pieces.shape[0]):
        pieces[i] = packed


def squares_tail(rows, lanes):
    total = jnp.sum(rows * rows, axis=1, keepdims=True)
    high, low = two_halves(total)
    lane = lax.broadcasted_iota(jnp.int32, (rows.shape[0], lanes), 1)
    first = jnp.where(lane == 0, high.astype(F32), 0.0)
    return jnp.where(lane == 1, low.astype(F32), first)


def cross_query_kernel(place, pieces, gain, weights, out):
    width = gain.shape[1] // XC
    rows = jnp.concatenate([unpack(pieces[i].astype(F32), width) for i in range(XC)], axis=1)
    tail = squares_tail(rows, 128)
    rows = (rows * gain[pl.ds(place[0], 1), :]).astype(BF)
    parts = [dot(rows, jnp.concatenate([weights[i] for i in range(Y)], axis=1))]
    by_line(jnp.concatenate(parts + [tail], axis=1), out)


def by_core(mine, near, far):
    own, other = near.astype(F32), far.astype(F32)
    return [jnp.where(mine == 0, own, other), jnp.where(mine == 0, other, own)]


def gate_up_kernel(
    place, near, far, gain, weights, out0, out1, out2, out3, rows, result
):
    hidden = weights.shape[1]
    width = gain.shape[1] // XC
    tails = []
    for i in range(Y):
        pieces = []
        for j in range(X):
            pieces += by_core(place[1], near[i * X + j], far[i * X + j])
        block = jnp.concatenate([unpack(piece, width) for piece in pieces], axis=1)
        here = pl.ds(i * ROWS, ROWS)
        tails.append(squares_tail(block, 128))
        rows[here, :] = (block * gain[pl.ds(place[0], 1), :]).astype(BF)
    gate = dot_t(rows[...], weights[0])
    up = dot_t(rows[...], weights[1])
    lane = lax.broadcasted_iota(jnp.int32, (ROWS, 128), 1)
    for i in range(Y):
        here = slice(i * ROWS, (i + 1) * ROWS)
        for j in range(3):
            part = slice(j * 128, (j + 1) * 128)
            result[i, j * ROWS : (j + 1) * ROWS, :] = gate[here, part].astype(BF)
            result[i, (j + 3) * ROWS : (j + 4) * ROWS, :] = up[here, part].astype(BF)
        last = tails[i]
        for j in range(384, hidden):
            last = jnp.where(lane == j - 384 + 2, gate[here, j : j + 1], last)
            last = jnp.where(lane == j - 384 + 4, up[here, j : j + 1], last)
        last = jnp.concatenate([last, jnp.zeros((128 - ROWS, 128), F32)], axis=0)
        result[i, 6 * ROWS :, :] = jnp.transpose(last)[:16].astype(BF)
    for shift, out in enumerate((out0, out1, out2, out3)):
        out[...] = result[pl.ds(lax.rem(place[0] + shift, Z), 1)][0]


def hidden_kernel(features, part0, part1, part2, part3, out):
    parts = part0[...].astype(F32) + part1[...].astype(F32)
    parts = parts + part2[...].astype(F32) + part3[...].astype(F32)
    last = jnp.concatenate([parts[6 * ROWS :], jnp.zeros((112, 128), F32)], axis=0)
    last = jnp.transpose(last)[:ROWS]
    scale = lax.rsqrt((last[:, 0:1] + last[:, 1:2]) / features + 1e-06)
    main = [parts[i * ROWS : (i + 1) * ROWS] for i in range(6)]
    gate = jnp.concatenate(main[:3] + [last[:, 2:4]], axis=1)
    up = jnp.concatenate(main[3:] + [last[:, 4:6]], axis=1)
    gate = (gate * scale).astype(BF).astype(F32)
    up = (up * scale).astype(BF).astype(F32)
    packed = pack(jax.nn.gelu(gate, approximate=True) * up).astype(BF)
    for i in range(X):
        out[i] = packed


def down_kernel(place, near, far, weights, state, out):
    pieces = []
    for j in range(X):
        pieces += by_core(place[1], near[j], far[j])
    width = weights.shape[2] // XC
    rows = jnp.concatenate([unpack(piece, width) for piece in pieces], axis=1).astype(BF)
    parts = []
    for i in range(Y):
        part = dot_t(rows, weights[i])
        parts.append(part + jnp.where(place[0] == i, state[...], 0.0))
    parts.append(jnp.zeros((ROWS, out.shape[2] - Y * state.shape[1]), F32))
    by_line(jnp.concatenate(parts, axis=1), out)


def logits_kernel(got, gain, head, out):
    width = gain.shape[1]
    block = width // XC
    total = summed(got, XC)
    main = head.shape[2]
    over = width - main
    squares = jnp.zeros((STEPS, 1), F32)
    sums = jnp.zeros((4 * STEPS, head.shape[1]), F32)
    for i in range(Y):
        rows = jnp.concatenate([part[:, i * block : (i + 1) * block] for part in total], axis=1)
        squares = squares + jnp.sum(rows * rows, axis=1, keepdims=True)
        rows = rows * gain[i : i + 1, :]
        stack = [rows[:, :main]]
        for j in range(3):
            pieces = [rows[:, main:], jnp.zeros((STEPS, main - (j + 1) * over), F32)]
            if j:
                pieces = [jnp.zeros((STEPS, j * over), F32)] + pieces
            stack.append(jnp.concatenate(pieces, axis=1))
        sums = sums + dot_t(jnp.concatenate(stack, axis=0).astype(BF), head[i])
    letters = out.shape[1] // (Y * XC)
    source = lax.broadcasted_iota(jnp.int32, (head.shape[1], out.shape[1]), 0)
    target = lax.broadcasted_iota(jnp.int32, (head.shape[1], out.shape[1]), 1)
    group, letter = target // letters * (letters * 4 // 3), target % letters
    logits = jnp.zeros((STEPS, out.shape[1]), F32)
    for i in range(4):
        if i == 0:
            keep = source == group + letter
        else:
            keep = (source == group + letters + letter // 3) & (letter % 3 == i - 1)
        keep = keep.astype(F32).astype(BF)
        high, low = two_halves(sums[i * STEPS : (i + 1) * STEPS])
        logits = logits + dot(high, keep) + dot(low, keep)
    scale = lax.rsqrt(squares / (width * Y) + 1e-06)
    out[...] = (logits * scale).astype(BF)


def turned(weights):
    parts = [weights]
    for shift in range(1, Y):
        pairs = [(i, (i - shift) % Y) for i in range(Y)]
        parts.append(lax.ppermute(weights, "y", pairs))
    return parts


def staged(weights):
    return call(copy_kernel, like(*weights.shape), weights)


def body(
    token_ids,
    mem_lengths,
    embed_table,
    w_qkv,
    w_self_out,
    w_cross_q,
    w_cross_out,
    w_in,
    w_out,
    lm_head,
    gain_self,
    gain_cross,
    gain_ffn,
    gain_final,
    self_keys,
    self_values,
    cross_keys,
    cross_values,
):
    z, y = lax.axis_index("z"), lax.axis_index("y")
    x, c = lax.axis_index("x"), lax.axis_index("c")
    vocab, width = embed_table.shape
    quarter = width // Z
    block = quarter // XC
    letters = lm_head.shape[1]
    place = jnp.stack([z, c, y])
    lines = ("z", "y", "x", "c")

    inner = self_keys.shape[3]
    self_out = lax.all_gather(w_self_out[0].T, "y")

    sibling = across(token_ids)
    pair = jnp.where(c == 0, jnp.stack([token_ids, sibling]), jnp.stack([sibling, token_ids]))
    tokens = jnp.broadcast_to(pair.reshape(1, C, STEPS), (Z * Y * X, C, STEPS))
    tokens, w_cross_q, w_out, lm_head = lax.optimization_barrier(
        (tokens, w_cross_q, w_out, lm_head)
    )
    cross_q = lax.all_gather(w_cross_q[0], "y")
    down = lax.all_gather(w_out[0].T, "y")
    head = lax.all_gather(call(head_kernel, like(letters * 4 // 3, 896), lm_head.T), lines)
    head = head.reshape(Z, -1, 896)
    tokens = swap(tokens, ("z", "y", "x"))
    tokens = tokens.reshape(Z * Y * X, C, STEPS)
    vocab_range = jnp.arange(vocab, dtype=jnp.int32)

    def one_hot(chosen):
        return (chosen.reshape(-1)[:, None] == vocab_range[None, :]).astype(BF)

    plane_tokens = lax.dynamic_index_in_dim(tokens.reshape(Z, Y, XC, STEPS), y, 1, keepdims=False)
    start = z * quarter + (x * C + c) * block
    own_block = lax.dynamic_slice_in_dim(embed_table, start, block, axis=1)
    state = dot(one_hot(plane_tokens), own_block)

    gain = lax.dynamic_slice_in_dim(gain_self[0], z * quarter, quarter)
    table = call(
        table_kernel,
        like(3 * 128, vocab),
        place,
        embed_table.T,
        jnp.broadcast_to(gain[:, None], (quarter, 128)),
        w_qkv[0].transpose(1, 0, 2),
        scalars=1,
    )
    pieces = call(
        pick_kernel, like(Z * PLANE, STEPS, 3 * 128), one_hot(tokens), table
    )
    got = swap(pieces, ("z", "y", "x", "c"))
    for_plane = like(PLANE, STEPS, inner // Z)
    pieces = call(self_kernel, for_plane, got, self_keys[0, 0], self_values[0, 0])

    got, self_out, w_in, w_cross_out = to_plane(pieces, self_out, w_in, w_cross_out)
    cross_out = turned(w_cross_out[0].T)
    weights = w_in[0].transpose(1, 2, 0)
    parts = swap(call(blocks_kernel, like(Y, PACKED, 128), got, staged(self_out)), "z")
    state, pieces = call(
        add_kernel, (like(ROWS, block, dtype=F32), like(XC, PACKED, 128)), parts, state
    )

    gain = gain_cross[0].reshape(Z, quarter)
    pieces, cross_q, *cross_out = lax.optimization_barrier((pieces, cross_q, *cross_out))
    pieces = swap(pieces, ("x", "c"))
    cross_q = staged(cross_q)
    parts = call(
        cross_query_kernel,
        like(PLANE, STEPS, (Y + 1) * 128),
        place,
        pieces,
        gain,
        cross_q,
        scalars=1,
    )
    parts, cross_values, cross_keys = lax.optimization_barrier(
        (parts, cross_values, cross_keys)
    )
    got = swap(parts, ("z", "x", "c"))
    pieces = call(
        lambda *refs: cross_kernel(width, *refs),
        for_plane,
        mem_lengths,
        got,
        cross_keys[0, 0, :128],
        cross_keys[0, 0, 128:],
        staged(cross_values[0, 0]),
        scalars=1,
    )

    got, = to_plane(pieces)
    parts = call(turned_blocks_kernel, like(Y, PACKED, 128), place, got, *cross_out, scalars=1)
    parts = swap(parts, "z")
    state, pieces = call(
        add_kernel, (like(ROWS, block, dtype=F32), like(Y * X, PACKED, 128)), parts, state
    )

    gain = gain_ffn[0].reshape(Z, quarter)
    pieces, down = lax.optimization_barrier((pieces, down))
    near = swap(pieces, ("y", "x"))
    down = staged(down)
    pieces = call(
        gate_up_kernel,
        [like(6 * ROWS + 16, 128)] * 4,
        place,
        near,
        across(near),
        gain,
        weights,
        scalars=1,
        scratch=(pltpu.VMEM((Z * ROWS, quarter), BF), pltpu.VMEM((Z, 6 * ROWS + 16, 128), BF)),
    )
    parts = []
    for shift in range(Z):
        pairs = [(i * Y + j, j * Y + (i + shift) % Z) for i in range(Z) for j in range(Y)]
        parts.append(lax.ppermute(pieces[shift], ("z", "y"), pairs))
    pieces = call(lambda *refs: hidden_kernel(width, *refs), like(X, PACKED, 384), *parts)

    near = swap(pieces, "x")
    parts = call(
        down_kernel,
        like(PLANE, STEPS, 640),
        place,
        near,
        across(near),
        down,
        state,
        scalars=1,
    )
    gain = gain_final.reshape(Z, quarter)
    got = swap(parts, ("z", "x", "c"))
    return call(logits_kernel, like(STEPS, vocab), got, gain, head)[:, None, :]


def solution(mesh):
    fine = Mesh(mesh.devices.reshape(Z, Y, X, C), ("z", "y", "x", "c"))
    lines = ("z", "y", "x", "c")
    columns = ("y", "x", "c")
    placed = (
        P(lines, None),
        P(lines),
        P(),
        P(None, "z", None, columns),
        P(None, "z", columns),
        P(None, "z", columns),
        P(None, "z", columns),
        P(None, "z", None, columns),
        P(None, "z", columns),
        P("z", columns),
        P(),
        P(),
        P(),
        P(),
        P(None, lines, None, None),
        P(None, lines, None, None),
        P(None, lines, None, None),
        P(None, lines, None, None),
    )
    return jax.shard_map(
        body, mesh=fine, in_specs=placed, out_specs=P(None, lines, None), check_vma=False
    )
```

```python
import jax
import jax.numpy as jnp
from jax import lax
from jax.experimental import pallas as pl
from jax.experimental.pallas import tpu as pltpu
from jax.sharding import Mesh, PartitionSpec as P

HEADS = 64
HEAD_DIM = 64
STEPS = 3
Z, Y, X, C = 4, 4, 4, 2
XC = X * C
PLANE = Z * XC
ROWS = PLANE * STEPS
GROUPS = ROWS // 16
PACKED = ROWS + 16
BF = jnp.bfloat16
F32 = jnp.float32
VMEM = pl.BlockSpec(memory_space=pltpu.VMEM)
SMEM = pl.BlockSpec(memory_space=pltpu.SMEM)


def swap(pieces, axes):
    return lax.all_to_all(pieces, axes, 0, 0, tiled=True)


def spread(block, count, axes):
    return swap(jnp.broadcast_to(block[None], (count,) + block.shape), axes)


def across(value):
    return lax.ppermute(value, "c", [(0, 1), (1, 0)])


def dot(a, b):
    return jnp.dot(a, b, preferred_element_type=F32)


def dot_t(a, b):
    return lax.dot_general(a, b, (((1,), (1,)), ((), ())), preferred_element_type=F32)


def two_halves(value):
    high = value.astype(BF)
    return high, (value - high.astype(F32)).astype(BF)


def call(kernel, out_shape, *operands, scalars=0, scratch=(), limit=24):
    return pl.pallas_call(
        kernel,
        out_shape=out_shape,
        in_specs=[SMEM] * scalars + [VMEM] * (len(operands) - scalars),
        out_specs=jax.tree.map(lambda _: VMEM, out_shape),
        scratch_shapes=list(scratch),
        compiler_params=pltpu.CompilerParams(vmem_limit_bytes=limit * 2**20),
        cost_estimate=pl.CostEstimate(flops=10**9, bytes_accessed=8 * 10**6, transcendentals=0),
    )(*operands)


def like(*shape, dtype=BF):
    return jax.ShapeDtypeStruct(shape, dtype)


def pack(rows):
    base = rows.shape[1] // 128 * 128
    tail = [rows[i * 16 : (i + 1) * 16, base:] for i in range(GROUPS)]
    empty = base - GROUPS * (rows.shape[1] - base)
    tail.append(jnp.zeros((16, empty), rows.dtype))
    return jnp.concatenate([rows[:, :base], jnp.concatenate(tail, axis=1)], axis=0)


def unpack(packed, width):
    over = width - packed.shape[1]
    tail = [packed[ROWS:, i * over : (i + 1) * over] for i in range(GROUPS)]
    return jnp.concatenate([packed[:ROWS], jnp.concatenate(tail, axis=0)], axis=1)


def by_line(rows, out):
    for i in range(out.shape[0]):
        out[i] = rows[i * STEPS : (i + 1) * STEPS].astype(out.dtype)


def line_rows(got):
    rows = [got[i].astype(F32) for i in range(got.shape[0])]
    return jnp.concatenate(rows, axis=0).astype(BF)


def summed(got, count):
    totals = []
    for i in range(count):
        part = got[i].astype(F32)
        for j in range(1, Z):
            part = part + got[j * count + i].astype(F32)
        totals.append(part)
    return totals


def head_mask(inner):
    heads = lax.broadcasted_iota(jnp.int32, (HEADS, inner), 0)
    owner = lax.broadcasted_iota(jnp.int32, (HEADS, inner), 1) // HEAD_DIM
    return heads == owner


def by_head(query, mask):
    rows = [jnp.where(mask, query[i : i + 1], 0.0).astype(BF) for i in range(STEPS)]
    return jnp.concatenate(rows, axis=0)


def store_attended(mixed, mask, out):
    rows = []
    for i in range(STEPS):
        kept = jnp.where(mask, mixed[i * HEADS : (i + 1) * HEADS], 0.0)
        rows.append(jnp.sum(kept, axis=0, keepdims=True))
    attended = jnp.concatenate(rows, axis=0).astype(BF)
    part = out.shape[2]
    for i in range(PLANE):
        j = i // XC
        out[i] = attended[:, j * part : (j + 1) * part]


def self_kernel(got, keys, values, out):
    triple = [[], [], []]
    for total in summed(got, PLANE):
        total = total.astype(BF).astype(F32)
        for i in range(3):
            triple[i].append(total[:, i * 128 : (i + 1) * 128])
    query, fresh_k, fresh_v = [jnp.concatenate(parts, axis=1) for parts in triple]
    inner = query.shape[1]
    empty = jnp.zeros((8 - STEPS, inner), F32)
    fresh_k = jnp.concatenate([fresh_k, empty], axis=0).astype(BF)
    fresh_v = jnp.concatenate([fresh_v, empty], axis=0).astype(BF)
    mask = head_mask(inner)
    wide = by_head(query, mask)
    step_of = lax.broadcasted_iota(jnp.int32, (STEPS * HEADS, 8), 0) // HEADS
    key_of = lax.broadcasted_iota(jnp.int32, (STEPS * HEADS, 8), 1)
    old = 0.125 * dot_t(wide, keys[...])
    new = jnp.where(key_of <= step_of, 0.125 * dot_t(wide, fresh_k), -jnp.inf)
    top = jnp.maximum(jnp.max(old, axis=1, keepdims=True), jnp.max(new, axis=1, keepdims=True))
    old, new = jnp.exp(old - top), jnp.exp(new - top)
    total = jnp.sum(old, axis=1, keepdims=True) + jnp.sum(new, axis=1, keepdims=True)
    mixed = dot((old / total).astype(BF), values[...]) + dot((new / total).astype(BF), fresh_v)
    store_attended(mixed, mask, out)


def cross_kernel(features, length, got, keys0, keys1, values, out):
    totals = summed(got, XC)
    inner = Y * 128
    squares = totals[0][:, inner : inner + 1] + totals[0][:, inner + 1 : inner + 2]
    scale = lax.rsqrt(squares / features + 1e-06)
    parts = [total[:, i * 128 : (i + 1) * 128] for i in range(Y) for total in totals]
    query = (jnp.concatenate(parts, axis=1) * scale).astype(BF).astype(F32)
    mask = head_mask(query.shape[1])
    wide = by_head(query, mask)
    scores = [0.125 * dot_t(wide, keys[...]) for keys in (keys0, keys1)]
    scores = jnp.concatenate(scores, axis=1)
    valid = lax.broadcasted_iota(jnp.int32, scores.shape, 1) < length[0]
    scores = jnp.where(valid, scores, -1e30)
    scores = jnp.exp(scores - jnp.max(scores, axis=1, keepdims=True))
    weights = (scores / jnp.sum(scores, axis=1, keepdims=True)).astype(BF)
    store_attended(dot(weights, values[...]), mask, out)


def to_plane(pieces, *early):
    pieces, *early = lax.optimization_barrier((pieces, *early))
    return swap(pieces, ("z", "x", "c")), *early


def pick_kernel(picked, table, out):
    by_line(dot_t(picked[...], table[...]), out)


def head_kernel(letters, out):
    count, width = letters.shape
    main = out.shape[1]
    rows = letters[...].astype(F32)
    tail = []
    for i in range(count // 3):
        pieces = [rows[3 * i + j : 3 * i + j + 1, main:] for j in range(3)]
        pieces.append(jnp.zeros((1, main - 3 * (width - main)), F32))
        tail.append(jnp.concatenate(pieces, axis=1))
    out[...] = jnp.concatenate([rows[:, :main]] + tail, axis=0).astype(BF)


def turned_blocks_kernel(place, got, own, next1, next2, next3, out):
    rows = line_rows(got)
    for i, weights in enumerate((own, next1, next2, next3)):
        block = pack(dot_t(rows, weights[...])).astype(BF)
        out[pl.ds(lax.rem(place[2] + i, Y), 1)] = block[None]


def copy_kernel(source, out):
    out[...] = source[...]


def table_kernel(place, table, gain, weight, out):
    features = table.shape[0]
    total = jnp.zeros((1, table.shape[1]), F32)
    quarter = weight.shape[1]
    for i in range(features // quarter):
        piece = table[pl.ds(i * quarter, quarter), :].astype(F32)
        total = total + jnp.sum(piece * piece, axis=0, keepdims=True)
    scale = lax.rsqrt(total / features + 1e-06)
    own = table[pl.ds(pl.multiple_of(place[0] * quarter, 16), quarter), :]
    for i in range(3):
        scaled = (weight[i].astype(F32) * gain[...]).astype(BF)
        part = lax.dot_general(scaled, own, (((0,), (0,)), ((), ())), preferred_element_type=F32)
        out[pl.ds(i * 128, 128), :] = (part * scale).astype(BF)


def blocks_kernel(got, weights, out):
    rows = line_rows(got)
    for i in range(Y):
        out[i] = pack(dot_t(rows, weights[i])).astype(BF)


def add_kernel(parts, state, new_state, pieces):
    total = parts[0].astype(F32) + parts[1].astype(F32) + parts[2].astype(F32) + parts[3].astype(F32)
    total = total.astype(BF).astype(F32)
    new = state[...] + unpack(total, state.shape[1])
    new_state[...] = new
    packed = pack(new).astype(BF)
    for i in range(pieces.shape[0]):
        pieces[i] = packed


def squares_tail(rows, lanes):
    total = jnp.sum(rows * rows, axis=1, keepdims=True)
    high, low = two_halves(total)
    lane = lax.broadcasted_iota(jnp.int32, (rows.shape[0], lanes), 1)
    first = jnp.where(lane == 0, high.astype(F32), 0.0)
    return jnp.where(lane == 1, low.astype(F32), first)


def cross_query_kernel(place, pieces, gain, weights, out):
    width = gain.shape[1] // XC
    rows = jnp.concatenate([unpack(pieces[i].astype(F32), width) for i in range(XC)], axis=1)
    tail = squares_tail(rows, 128)
    rows = (rows * gain[pl.ds(place[0], 1), :]).astype(BF)
    parts = [dot(rows, jnp.concatenate([weights[i] for i in range(Y)], axis=1))]
    by_line(jnp.concatenate(parts + [tail], axis=1), out)


def by_core(mine, near, far):
    own, other = near.astype(F32), far.astype(F32)
    return [jnp.where(mine == 0, own, other), jnp.where(mine == 0, other, own)]


def gate_up_kernel(
    place, near, far, gain, weights, out0, out1, out2, out3, rows, result
):
    hidden = weights.shape[1]
    width = gain.shape[1] // XC
    tails = []
    for i in range(Y):
        pieces = []
        for j in range(X):
            pieces += by_core(place[1], near[i * X + j], far[i * X + j])
        block = jnp.concatenate([unpack(piece, width) for piece in pieces], axis=1)
        here = pl.ds(i * ROWS, ROWS)
        tails.append(squares_tail(block, 128))
        rows[here, :] = (block * gain[pl.ds(place[0], 1), :]).astype(BF)
    gate = dot_t(rows[...], weights[0])
    up = dot_t(rows[...], weights[1])
    lane = lax.broadcasted_iota(jnp.int32, (ROWS, 128), 1)
    for i in range(Y):
        here = slice(i * ROWS, (i + 1) * ROWS)
        for j in range(3):
            part = slice(j * 128, (j + 1) * 128)
            result[i, j * ROWS : (j + 1) * ROWS, :] = gate[here, part].astype(BF)
            result[i, (j + 3) * ROWS : (j + 4) * ROWS, :] = up[here, part].astype(BF)
        last = tails[i]
        for j in range(384, hidden):
            last = jnp.where(lane == j - 384 + 2, gate[here, j : j + 1], last)
            last = jnp.where(lane == j - 384 + 4, up[here, j : j + 1], last)
        last = jnp.concatenate([last, jnp.zeros((128 - ROWS, 128), F32)], axis=0)
        result[i, 6 * ROWS :, :] = jnp.transpose(last)[:16].astype(BF)
    for shift, out in enumerate((out0, out1, out2, out3)):
        out[...] = result[pl.ds(lax.rem(place[0] + shift, Z), 1)][0]


def hidden_kernel(features, part0, part1, part2, part3, out):
    parts = part0[...].astype(F32) + part1[...].astype(F32)
    parts = parts + part2[...].astype(F32) + part3[...].astype(F32)
    last = jnp.concatenate([parts[6 * ROWS :], jnp.zeros((112, 128), F32)], axis=0)
    last = jnp.transpose(last)[:ROWS]
    scale = lax.rsqrt((last[:, 0:1] + last[:, 1:2]) / features + 1e-06)
    main = [parts[i * ROWS : (i + 1) * ROWS] for i in range(6)]
    gate = jnp.concatenate(main[:3] + [last[:, 2:4]], axis=1)
    up = jnp.concatenate(main[3:] + [last[:, 4:6]], axis=1)
    gate = (gate * scale).astype(BF).astype(F32)
    up = (up * scale).astype(BF).astype(F32)
    packed = pack(jax.nn.gelu(gate, approximate=True) * up).astype(BF)
    for i in range(X):
        out[i] = packed


def down_kernel(place, near, far, weights, state, out):
    pieces = []
    for j in range(X):
        pieces += by_core(place[1], near[j], far[j])
    width = weights.shape[2] // XC
    rows = jnp.concatenate([unpack(piece, width) for piece in pieces], axis=1).astype(BF)
    parts = []
    for i in range(Y):
        part = dot_t(rows, weights[i])
        parts.append(part + jnp.where(place[0] == i, state[...], 0.0))
    parts.append(jnp.zeros((ROWS, out.shape[2] - Y * state.shape[1]), F32))
    by_line(jnp.concatenate(parts, axis=1), out)


def logits_kernel(got, gain, head, out):
    width = gain.shape[1]
    block = width // XC
    total = summed(got, XC)
    main = head.shape[2]
    over = width - main
    squares = jnp.zeros((STEPS, 1), F32)
    sums = jnp.zeros((4 * STEPS, head.shape[1]), F32)
    for i in range(Y):
        rows = jnp.concatenate([part[:, i * block : (i + 1) * block] for part in total], axis=1)
        squares = squares + jnp.sum(rows * rows, axis=1, keepdims=True)
        rows = rows * gain[i : i + 1, :]
        stack = [rows[:, :main]]
        for j in range(3):
            pieces = [rows[:, main:], jnp.zeros((STEPS, main - (j + 1) * over), F32)]
            if j:
                pieces = [jnp.zeros((STEPS, j * over), F32)] + pieces
            stack.append(jnp.concatenate(pieces, axis=1))
        sums = sums + dot_t(jnp.concatenate(stack, axis=0).astype(BF), head[i])
    letters = out.shape[1] // (Y * XC)
    source = lax.broadcasted_iota(jnp.int32, (head.shape[1], out.shape[1]), 0)
    target = lax.broadcasted_iota(jnp.int32, (head.shape[1], out.shape[1]), 1)
    group, letter = target // letters * (letters * 4 // 3), target % letters
    logits = jnp.zeros((STEPS, out.shape[1]), F32)
    for i in range(4):
        if i == 0:
            keep = source == group + letter
        else:
            keep = (source == group + letters + letter // 3) & (letter % 3 == i - 1)
        keep = keep.astype(F32).astype(BF)
        high, low = two_halves(sums[i * STEPS : (i + 1) * STEPS])
        logits = logits + dot(high, keep) + dot(low, keep)
    scale = lax.rsqrt(squares / (width * Y) + 1e-06)
    out[...] = (logits * scale).astype(BF)


def turned(weights):
    parts = [weights]
    for shift in range(1, Y):
        pairs = [(i, (i - shift) % Y) for i in range(Y)]
        parts.append(lax.ppermute(weights, "y", pairs))
    return parts


def staged(weights):
    return call(copy_kernel, like(*weights.shape), weights)


def body(
    token_ids,
    mem_lengths,
    embed_table,
    w_qkv,
    w_self_out,
    w_cross_q,
    w_cross_out,
    w_in,
    w_out,
    lm_head,
    gain_self,
    gain_cross,
    gain_ffn,
    gain_final,
    self_keys,
    self_values,
    cross_keys,
    cross_values,
):
    z, y = lax.axis_index("z"), lax.axis_index("y")
    x, c = lax.axis_index("x"), lax.axis_index("c")
    vocab, width = embed_table.shape
    quarter = width // Z
    block = quarter // XC
    letters = lm_head.shape[1]
    place = jnp.stack([z, c, y])
    lines = ("z", "y", "x", "c")

    inner = self_keys.shape[3]
    self_out = lax.all_gather(w_self_out[0].T, "y")

    sibling = across(token_ids)
    pair = jnp.where(c == 0, jnp.stack([token_ids, sibling]), jnp.stack([sibling, token_ids]))
    tokens = jnp.broadcast_to(pair.reshape(1, C, STEPS), (Z * Y * X, C, STEPS))
    tokens, w_cross_q, w_out, lm_head = lax.optimization_barrier(
        (tokens, w_cross_q, w_out, lm_head)
    )
    cross_q = lax.all_gather(w_cross_q[0], "y")
    down = lax.all_gather(w_out[0].T, "y")
    head = lax.all_gather(call(head_kernel, like(letters * 4 // 3, 896), lm_head.T), lines)
    head = head.reshape(Z, -1, 896)
    tokens = swap(tokens, ("z", "y", "x"))
    tokens = tokens.reshape(Z * Y * X, C, STEPS)
    vocab_range = jnp.arange(vocab, dtype=jnp.int32)

    def one_hot(chosen):
        return (chosen.reshape(-1)[:, None] == vocab_range[None, :]).astype(BF)

    plane_tokens = lax.dynamic_index_in_dim(tokens.reshape(Z, Y, XC, STEPS), y, 1, keepdims=False)
    start = z * quarter + (x * C + c) * block
    own_block = lax.dynamic_slice_in_dim(embed_table, start, block, axis=1)
    state = dot(one_hot(plane_tokens), own_block)

    gain = lax.dynamic_slice_in_dim(gain_self[0], z * quarter, quarter)
    table = call(
        table_kernel,
        like(3 * 128, vocab),
        place,
        embed_table.T,
        jnp.broadcast_to(gain[:, None], (quarter, 128)),
        w_qkv[0].transpose(1, 0, 2),
        scalars=1,
    )
    pieces = call(
        pick_kernel, like(Z * PLANE, STEPS, 3 * 128), one_hot(tokens), table
    )
    got = swap(pieces, ("z", "y", "x", "c"))
    for_plane = like(PLANE, STEPS, inner // Z)
    pieces = call(self_kernel, for_plane, got, self_keys[0, 0], self_values[0, 0])

    got, self_out, w_in, w_cross_out = to_plane(pieces, self_out, w_in, w_cross_out)
    cross_out = turned(w_cross_out[0].T)
    weights = w_in[0].transpose(1, 2, 0)
    parts = swap(call(blocks_kernel, like(Y, PACKED, 128), got, staged(self_out)), "z")
    state, pieces = call(
        add_kernel, (like(ROWS, block, dtype=F32), like(XC, PACKED, 128)), parts, state
    )

    gain = gain_cross[0].reshape(Z, quarter)
    pieces, cross_q, *cross_out = lax.optimization_barrier((pieces, cross_q, *cross_out))
    pieces = swap(pieces, ("x", "c"))
    cross_q = staged(cross_q)
    parts = call(
        cross_query_kernel,
        like(PLANE, STEPS, (Y + 1) * 128),
        place,
        pieces,
        gain,
        cross_q,
        scalars=1,
    )
    parts, cross_values, cross_keys = lax.optimization_barrier(
        (parts, cross_values, cross_keys)
    )
    got = swap(parts, ("z", "x", "c"))
    pieces = call(
        lambda *refs: cross_kernel(width, *refs),
        for_plane,
        mem_lengths,
        got,
        cross_keys[0, 0, :128],
        cross_keys[0, 0, 128:],
        staged(cross_values[0, 0]),
        scalars=1,
    )

    got, = to_plane(pieces)
    parts = call(turned_blocks_kernel, like(Y, PACKED, 128), place, got, *cross_out, scalars=1)
    parts = swap(parts, "z")
    state, pieces = call(
        add_kernel, (like(ROWS, block, dtype=F32), like(Y * X, PACKED, 128)), parts, state
    )

    gain = gain_ffn[0].reshape(Z, quarter)
    pieces, down = lax.optimization_barrier((pieces, down))
    near = swap(pieces, ("y", "x"))
    down = staged(down)
    pieces = call(
        gate_up_kernel,
        [like(6 * ROWS + 16, 128)] * 4,
        place,
        near,
        across(near),
        gain,
        weights,
        scalars=1,
        scratch=(pltpu.VMEM((Z * ROWS, quarter), BF), pltpu.VMEM((Z, 6 * ROWS + 16, 128), BF)),
    )
    parts = []
    for shift in range(Z):
        pairs = [(i * Y + j, j * Y + (i + shift) % Z) for i in range(Z) for j in range(Y)]
        parts.append(lax.ppermute(pieces[shift], ("z", "y"), pairs))
    pieces = call(lambda *refs: hidden_kernel(width, *refs), like(X, PACKED, 384), *parts)

    near = swap(pieces, "x")
    parts = call(
        down_kernel,
        like(PLANE, STEPS, 640),
        place,
        near,
        across(near),
        down,
        state,
        scalars=1,
    )
    gain = gain_final.reshape(Z, quarter)
    got = swap(parts, ("z", "x", "c"))
    return call(logits_kernel, like(STEPS, vocab), got, gain, head)[:, None, :]


def solution(mesh):
    fine = Mesh(mesh.devices.reshape(Z, Y, X, C), ("z", "y", "x", "c"))
    lines = ("z", "y", "x", "c")
    columns = ("y", "x", "c")
    placed = (
        P(lines, None),
        P(lines),
        P(),
        P(None, "z", None, columns),
        P(None, "z", columns),
        P(None, "z", columns),
        P(None, "z", columns),
        P(None, "z", None, columns),
        P(None, "z", columns),
        P("z", columns),
        P(),
        P(),
        P(),
        P(),
        P(None, lines, None, None),
        P(None, lines, None, None),
        P(None, lines, None, None),
        P(None, lines, None, None),
    )
    return jax.shard_map(
        body, mesh=fine, in_specs=placed, out_specs=P(None, lines, None), check_vma=False
    )
```

```python
import jax
import jax.numpy as jnp
from jax import lax
from jax.experimental import pallas as pl
from jax.experimental.pallas import tpu as pltpu
from jax.sharding import Mesh, PartitionSpec as P

HEADS = 64
HEAD_DIM = 64
STEPS = 3
Z, Y, X, C = 4, 4, 4, 2
XC = X * C
PLANE = Z * XC
ROWS = PLANE * STEPS
GROUPS = ROWS // 16
PACKED = ROWS + 16
BF = jnp.bfloat16
F32 = jnp.float32
VMEM = pl.BlockSpec(memory_space=pltpu.VMEM)
SMEM = pl.BlockSpec(memory_space=pltpu.SMEM)


def swap(pieces, axes):
    return lax.all_to_all(pieces, axes, 0, 0, tiled=True)


def spread(block, count, axes):
    return swap(jnp.broadcast_to(block[None], (count,) + block.shape), axes)


def across(value):
    return lax.ppermute(value, "c", [(0, 1), (1, 0)])


def dot(a, b):
    return jnp.dot(a, b, preferred_element_type=F32)


def dot_t(a, b):
    return lax.dot_general(a, b, (((1,), (1,)), ((), ())), preferred_element_type=F32)


def two_halves(value):
    high = value.astype(BF)
    return high, (value - high.astype(F32)).astype(BF)


def call(kernel, out_shape, *operands, scalars=0, scratch=(), limit=24):
    return pl.pallas_call(
        kernel,
        out_shape=out_shape,
        in_specs=[SMEM] * scalars + [VMEM] * (len(operands) - scalars),
        out_specs=jax.tree.map(lambda _: VMEM, out_shape),
        scratch_shapes=list(scratch),
        compiler_params=pltpu.CompilerParams(vmem_limit_bytes=limit * 2**20),
        cost_estimate=pl.CostEstimate(flops=10**9, bytes_accessed=8 * 10**6, transcendentals=0),
    )(*operands)


def like(*shape, dtype=BF):
    return jax.ShapeDtypeStruct(shape, dtype)


def pack(rows):
    base = rows.shape[1] // 128 * 128
    tail = [rows[i * 16 : (i + 1) * 16, base:] for i in range(GROUPS)]
    empty = base - GROUPS * (rows.shape[1] - base)
    tail.append(jnp.zeros((16, empty), rows.dtype))
    return jnp.concatenate([rows[:, :base], jnp.concatenate(tail, axis=1)], axis=0)


def unpack(packed, width):
    over = width - packed.shape[1]
    tail = [packed[ROWS:, i * over : (i + 1) * over] for i in range(GROUPS)]
    return jnp.concatenate([packed[:ROWS], jnp.concatenate(tail, axis=0)], axis=1)


def by_line(rows, out):
    for i in range(out.shape[0]):
        out[i] = rows[i * STEPS : (i + 1) * STEPS].astype(out.dtype)


def line_rows(got):
    rows = [got[i].astype(F32) for i in range(got.shape[0])]
    return jnp.concatenate(rows, axis=0).astype(BF)


def summed(got, count):
    totals = []
    for i in range(count):
        part = got[i].astype(F32)
        for j in range(1, Z):
            part = part + got[j * count + i].astype(F32)
        totals.append(part)
    return totals


def head_mask(inner):
    heads = lax.broadcasted_iota(jnp.int32, (HEADS, inner), 0)
    owner = lax.broadcasted_iota(jnp.int32, (HEADS, inner), 1) // HEAD_DIM
    return heads == owner


def by_head(query, mask):
    rows = [jnp.where(mask, query[i : i + 1], 0.0).astype(BF) for i in range(STEPS)]
    return jnp.concatenate(rows, axis=0)


def store_attended(mixed, mask, out):
    rows = []
    for i in range(STEPS):
        kept = jnp.where(mask, mixed[i * HEADS : (i + 1) * HEADS], 0.0)
        rows.append(jnp.sum(kept, axis=0, keepdims=True))
    attended = jnp.concatenate(rows, axis=0).astype(BF)
    part = out.shape[2]
    for i in range(PLANE):
        j = i // XC
        out[i] = attended[:, j * part : (j + 1) * part]


def self_kernel(got, keys, values, out):
    triple = [[], [], []]
    for total in summed(got, PLANE):
        total = total.astype(BF).astype(F32)
        for i in range(3):
            triple[i].append(total[:, i * 128 : (i + 1) * 128])
    query, fresh_k, fresh_v = [jnp.concatenate(parts, axis=1) for parts in triple]
    inner = query.shape[1]
    empty = jnp.zeros((8 - STEPS, inner), F32)
    fresh_k = jnp.concatenate([fresh_k, empty], axis=0).astype(BF)
    fresh_v = jnp.concatenate([fresh_v, empty], axis=0).astype(BF)
    mask = head_mask(inner)
    wide = by_head(query, mask)
    step_of = lax.broadcasted_iota(jnp.int32, (STEPS * HEADS, 8), 0) // HEADS
    key_of = lax.broadcasted_iota(jnp.int32, (STEPS * HEADS, 8), 1)
    old = 0.125 * dot_t(wide, keys[...])
    new = jnp.where(key_of <= step_of, 0.125 * dot_t(wide, fresh_k), -jnp.inf)
    top = jnp.maximum(jnp.max(old, axis=1, keepdims=True), jnp.max(new, axis=1, keepdims=True))
    old, new = jnp.exp(old - top), jnp.exp(new - top)
    total = jnp.sum(old, axis=1, keepdims=True) + jnp.sum(new, axis=1, keepdims=True)
    mixed = dot((old / total).astype(BF), values[...]) + dot((new / total).astype(BF), fresh_v)
    store_attended(mixed, mask, out)


def cross_kernel(features, length, got, keys0, keys1, values0, values1, out):
    totals = summed(got, XC)
    inner = Y * 128
    squares = totals[0][:, inner : inner + 1] + totals[0][:, inner + 1 : inner + 2]
    scale = lax.rsqrt(squares / features + 1e-06)
    parts = [total[:, i * 128 : (i + 1) * 128] for i in range(Y) for total in totals]
    query = (jnp.concatenate(parts, axis=1) * scale).astype(BF).astype(F32)
    mask = head_mask(query.shape[1])
    wide = by_head(query, mask)
    scores = [0.125 * dot_t(wide, keys[...]) for keys in (keys0, keys1)]
    scores = jnp.concatenate(scores, axis=1)
    valid = lax.broadcasted_iota(jnp.int32, scores.shape, 1) < length[0]
    scores = jnp.where(valid, scores, -1e30)
    scores = jnp.exp(scores - jnp.max(scores, axis=1, keepdims=True))
    weights = (scores / jnp.sum(scores, axis=1, keepdims=True)).astype(BF)
    mixed = dot(weights[:, :128], values0[...]) + dot(weights[:, 128:], values1[...])
    store_attended(mixed, mask, out)


def to_plane(pieces, *early):
    pieces, *early = lax.optimization_barrier((pieces, *early))
    return swap(pieces, ("z", "x", "c")), *early


def pick_kernel(picked, table, out):
    by_line(dot_t(picked[...], table[...]), out)


def head_kernel(letters, out):
    count, width = letters.shape
    main = out.shape[1]
    rows = letters[...].astype(F32)
    tail = []
    for i in range(count // 3):
        pieces = [rows[3 * i + j : 3 * i + j + 1, main:] for j in range(3)]
        pieces.append(jnp.zeros((1, main - 3 * (width - main)), F32))
        tail.append(jnp.concatenate(pieces, axis=1))
    out[...] = jnp.concatenate([rows[:, :main]] + tail, axis=0).astype(BF)


def turned_blocks_kernel(place, got, own, next1, next2, next3, out):
    rows = line_rows(got)
    for i, weights in enumerate((own, next1, next2, next3)):
        block = pack(dot_t(rows, weights[...])).astype(BF)
        out[pl.ds(lax.rem(place[2] + i, Y), 1)] = block[None]


def copy_kernel(source, out):
    out[...] = source[...]


def table_kernel(place, table, gain, weight, out):
    features = table.shape[0]
    total = jnp.zeros((1, table.shape[1]), F32)
    quarter = weight.shape[1]
    for i in range(features // quarter):
        piece = table[pl.ds(i * quarter, quarter), :].astype(F32)
        total = total + jnp.sum(piece * piece, axis=0, keepdims=True)
    scale = lax.rsqrt(total / features + 1e-06)
    own = table[pl.ds(pl.multiple_of(place[0] * quarter, 16), quarter), :]
    for i in range(3):
        scaled = (weight[i].astype(F32) * gain[...]).astype(BF)
        part = lax.dot_general(scaled, own, (((0,), (0,)), ((), ())), preferred_element_type=F32)
        out[pl.ds(i * 128, 128), :] = (part * scale).astype(BF)


def blocks_kernel(got, weights, out):
    rows = line_rows(got)
    for i in range(Y):
        out[i] = pack(dot_t(rows, weights[i])).astype(BF)


def add_kernel(parts, state, new_state, pieces):
    total = parts[0].astype(F32) + parts[1].astype(F32) + parts[2].astype(F32) + parts[3].astype(F32)
    total = total.astype(BF).astype(F32)
    new = state[...] + unpack(total, state.shape[1])
    new_state[...] = new
    packed = pack(new).astype(BF)
    for i in range(pieces.shape[0]):
        pieces[i] = packed


def squares_tail(rows, lanes):
    total = jnp.sum(rows * rows, axis=1, keepdims=True)
    high, low = two_halves(total)
    lane = lax.broadcasted_iota(jnp.int32, (rows.shape[0], lanes), 1)
    first = jnp.where(lane == 0, high.astype(F32), 0.0)
    return jnp.where(lane == 1, low.astype(F32), first)


def cross_query_kernel(place, pieces, gain, weights, out):
    width = gain.shape[1] // XC
    rows = jnp.concatenate([unpack(pieces[i].astype(F32), width) for i in range(XC)], axis=1)
    tail = squares_tail(rows, 128)
    rows = (rows * gain[pl.ds(place[0], 1), :]).astype(BF)
    parts = [dot(rows, jnp.concatenate([weights[i] for i in range(Y)], axis=1))]
    by_line(jnp.concatenate(parts + [tail], axis=1), out)


def by_core(mine, near, far):
    own, other = near.astype(F32), far.astype(F32)
    return [jnp.where(mine == 0, own, other), jnp.where(mine == 0, other, own)]


def gate_up_kernel(
    place, near, far, gain, weights, out0, out1, out2, out3, rows, result
):
    hidden = weights.shape[1]
    width = gain.shape[1] // XC
    tails = []
    for i in range(Y):
        pieces = []
        for j in range(X):
            pieces += by_core(place[1], near[i * X + j], far[i * X + j])
        block = jnp.concatenate([unpack(piece, width) for piece in pieces], axis=1)
        here = pl.ds(i * ROWS, ROWS)
        tails.append(squares_tail(block, 128))
        rows[here, :] = (block * gain[pl.ds(place[0], 1), :]).astype(BF)
    gate = dot_t(rows[...], weights[0])
    up = dot_t(rows[...], weights[1])
    lane = lax.broadcasted_iota(jnp.int32, (ROWS, 128), 1)
    for i in range(Y):
        here = slice(i * ROWS, (i + 1) * ROWS)
        for j in range(3):
            part = slice(j * 128, (j + 1) * 128)
            result[i, j * ROWS : (j + 1) * ROWS, :] = gate[here, part].astype(BF)
            result[i, (j + 3) * ROWS : (j + 4) * ROWS, :] = up[here, part].astype(BF)
        last = tails[i]
        for j in range(384, hidden):
            last = jnp.where(lane == j - 384 + 2, gate[here, j : j + 1], last)
            last = jnp.where(lane == j - 384 + 4, up[here, j : j + 1], last)
        last = jnp.concatenate([last, jnp.zeros((128 - ROWS, 128), F32)], axis=0)
        result[i, 6 * ROWS :, :] = jnp.transpose(last)[:16].astype(BF)
    for shift, out in enumerate((out0, out1, out2, out3)):
        out[...] = result[pl.ds(lax.rem(place[0] + shift, Z), 1)][0]


def hidden_kernel(features, part0, part1, part2, part3, out):
    parts = part0[...].astype(F32) + part1[...].astype(F32)
    parts = parts + part2[...].astype(F32) + part3[...].astype(F32)
    last = jnp.concatenate([parts[6 * ROWS :], jnp.zeros((112, 128), F32)], axis=0)
    last = jnp.transpose(last)[:ROWS]
    scale = lax.rsqrt((last[:, 0:1] + last[:, 1:2]) / features + 1e-06)
    main = [parts[i * ROWS : (i + 1) * ROWS] for i in range(6)]
    gate = jnp.concatenate(main[:3] + [last[:, 2:4]], axis=1)
    up = jnp.concatenate(main[3:] + [last[:, 4:6]], axis=1)
    gate = (gate * scale).astype(BF).astype(F32)
    up = (up * scale).astype(BF).astype(F32)
    packed = pack(jax.nn.gelu(gate, approximate=True) * up).astype(BF)
    for i in range(X):
        out[i] = packed


def down_kernel(place, near, far, weights, state, out):
    pieces = []
    for j in range(X):
        pieces += by_core(place[1], near[j], far[j])
    width = weights.shape[2] // XC
    rows = jnp.concatenate([unpack(piece, width) for piece in pieces], axis=1).astype(BF)
    parts = []
    for i in range(Y):
        part = dot_t(rows, weights[i])
        parts.append(part + jnp.where(place[0] == i, state[...], 0.0))
    parts.append(jnp.zeros((ROWS, out.shape[2] - Y * state.shape[1]), F32))
    by_line(jnp.concatenate(parts, axis=1), out)


def logits_kernel(got, gain, head, out):
    width = gain.shape[1]
    block = width // XC
    total = summed(got, XC)
    main = head.shape[2]
    over = width - main
    squares = jnp.zeros((STEPS, 1), F32)
    sums = jnp.zeros((4 * STEPS, head.shape[1]), F32)
    for i in range(Y):
        rows = jnp.concatenate([part[:, i * block : (i + 1) * block] for part in total], axis=1)
        squares = squares + jnp.sum(rows * rows, axis=1, keepdims=True)
        rows = rows * gain[i : i + 1, :]
        stack = [rows[:, :main]]
        for j in range(3):
            pieces = [rows[:, main:], jnp.zeros((STEPS, main - (j + 1) * over), F32)]
            if j:
                pieces = [jnp.zeros((STEPS, j * over), F32)] + pieces
            stack.append(jnp.concatenate(pieces, axis=1))
        sums = sums + dot_t(jnp.concatenate(stack, axis=0).astype(BF), head[i])
    letters = out.shape[1] // (Y * XC)
    source = lax.broadcasted_iota(jnp.int32, (head.shape[1], out.shape[1]), 0)
    target = lax.broadcasted_iota(jnp.int32, (head.shape[1], out.shape[1]), 1)
    group, letter = target // letters * (letters * 4 // 3), target % letters
    logits = jnp.zeros((STEPS, out.shape[1]), F32)
    for i in range(4):
        if i == 0:
            keep = source == group + letter
        else:
            keep = (source == group + letters + letter // 3) & (letter % 3 == i - 1)
        keep = keep.astype(F32).astype(BF)
        high, low = two_halves(sums[i * STEPS : (i + 1) * STEPS])
        logits = logits + dot(high, keep) + dot(low, keep)
    scale = lax.rsqrt(squares / (width * Y) + 1e-06)
    out[...] = (logits * scale).astype(BF)


def turned(weights):
    parts = [weights]
    for shift in range(1, Y):
        pairs = [(i, (i - shift) % Y) for i in range(Y)]
        parts.append(lax.ppermute(weights, "y", pairs))
    return parts


def staged(weights):
    return call(copy_kernel, like(*weights.shape), weights)


def body(
    token_ids,
    mem_lengths,
    embed_table,
    w_qkv,
    w_self_out,
    w_cross_q,
    w_cross_out,
    w_in,
    w_out,
    lm_head,
    gain_self,
    gain_cross,
    gain_ffn,
    gain_final,
    self_keys,
    self_values,
    cross_keys,
    cross_values,
):
    z, y = lax.axis_index("z"), lax.axis_index("y")
    x, c = lax.axis_index("x"), lax.axis_index("c")
    vocab, width = embed_table.shape
    quarter = width // Z
    block = quarter // XC
    letters = lm_head.shape[1]
    place = jnp.stack([z, c, y])
    lines = ("z", "y", "x", "c")

    inner = self_keys.shape[3]
    self_out = lax.all_gather(w_self_out[0].T, "y")

    sibling = across(token_ids)
    pair = jnp.where(c == 0, jnp.stack([token_ids, sibling]), jnp.stack([sibling, token_ids]))
    tokens = jnp.broadcast_to(pair.reshape(1, C, STEPS), (Z * Y * X, C, STEPS))
    tokens, w_cross_q, w_out, lm_head = lax.optimization_barrier(
        (tokens, w_cross_q, w_out, lm_head)
    )
    cross_q = lax.all_gather(w_cross_q[0], "y")
    down = lax.all_gather(w_out[0].T, "y")
    head = lax.all_gather(call(head_kernel, like(letters * 4 // 3, 896), lm_head.T), lines)
    head = head.reshape(Z, -1, 896)
    tokens = swap(tokens, ("z", "y", "x"))
    tokens = tokens.reshape(Z * Y * X, C, STEPS)
    vocab_range = jnp.arange(vocab, dtype=jnp.int32)

    def one_hot(chosen):
        return (chosen.reshape(-1)[:, None] == vocab_range[None, :]).astype(BF)

    plane_tokens = lax.dynamic_index_in_dim(tokens.reshape(Z, Y, XC, STEPS), y, 1, keepdims=False)
    start = z * quarter + (x * C + c) * block
    own_block = lax.dynamic_slice_in_dim(embed_table, start, block, axis=1)
    state = dot(one_hot(plane_tokens), own_block)

    gain = lax.dynamic_slice_in_dim(gain_self[0], z * quarter, quarter)
    table = call(
        table_kernel,
        like(3 * 128, vocab),
        place,
        embed_table.T,
        jnp.broadcast_to(gain[:, None], (quarter, 128)),
        w_qkv[0].transpose(1, 0, 2),
        scalars=1,
    )
    pieces = call(
        pick_kernel, like(Z * PLANE, STEPS, 3 * 128), one_hot(tokens), table
    )
    got = swap(pieces, ("z", "y", "x", "c"))
    for_plane = like(PLANE, STEPS, inner // Z)
    pieces = call(self_kernel, for_plane, got, self_keys[0, 0], self_values[0, 0])

    got, self_out, w_in, w_cross_out = to_plane(pieces, self_out, w_in, w_cross_out)
    cross_out = turned(w_cross_out[0].T)
    weights = w_in[0].transpose(1, 2, 0)
    parts = swap(call(blocks_kernel, like(Y, PACKED, 128), got, staged(self_out)), "z")
    state, pieces = call(
        add_kernel, (like(ROWS, block, dtype=F32), like(XC, PACKED, 128)), parts, state
    )

    gain = gain_cross[0].reshape(Z, quarter)
    pieces, cross_q, *cross_out = lax.optimization_barrier((pieces, cross_q, *cross_out))
    pieces = swap(pieces, ("x", "c"))
    cross_q = staged(cross_q)
    parts = call(
        cross_query_kernel,
        like(PLANE, STEPS, (Y + 1) * 128),
        place,
        pieces,
        gain,
        cross_q,
        scalars=1,
    )
    parts, cross_values, cross_keys = lax.optimization_barrier(
        (parts, cross_values, cross_keys)
    )
    got = swap(parts, ("z", "x", "c"))
    pieces = call(
        lambda *refs: cross_kernel(width, *refs),
        for_plane,
        mem_lengths,
        got,
        cross_keys[0, 0, :128],
        cross_keys[0, 0, 128:],
        cross_values[0, 0, :128],
        cross_values[0, 0, 128:],
        scalars=1,
    )

    got, = to_plane(pieces)
    parts = call(turned_blocks_kernel, like(Y, PACKED, 128), place, got, *cross_out, scalars=1)
    parts = swap(parts, "z")
    state, pieces = call(
        add_kernel, (like(ROWS, block, dtype=F32), like(Y * X, PACKED, 128)), parts, state
    )

    gain = gain_ffn[0].reshape(Z, quarter)
    pieces, down = lax.optimization_barrier((pieces, down))
    near = swap(pieces, ("y", "x"))
    down = staged(down)
    pieces = call(
        gate_up_kernel,
        [like(6 * ROWS + 16, 128)] * 4,
        place,
        near,
        across(near),
        gain,
        weights,
        scalars=1,
        scratch=(pltpu.VMEM((Z * ROWS, quarter), BF), pltpu.VMEM((Z, 6 * ROWS + 16, 128), BF)),
    )
    parts = []
    for shift in range(Z):
        pairs = [(i * Y + j, j * Y + (i + shift) % Z) for i in range(Z) for j in range(Y)]
        parts.append(lax.ppermute(pieces[shift], ("z", "y"), pairs))
    pieces = call(lambda *refs: hidden_kernel(width, *refs), like(X, PACKED, 384), *parts)

    near = swap(pieces, "x")
    parts = call(
        down_kernel,
        like(PLANE, STEPS, 640),
        place,
        near,
        across(near),
        down,
        state,
        scalars=1,
    )
    gain = gain_final.reshape(Z, quarter)
    got = swap(parts, ("z", "x", "c"))
    return call(logits_kernel, like(STEPS, vocab), got, gain, head)[:, None, :]


def solution(mesh):
    fine = Mesh(mesh.devices.reshape(Z, Y, X, C), ("z", "y", "x", "c"))
    lines = ("z", "y", "x", "c")
    columns = ("y", "x", "c")
    placed = (
        P(lines, None),
        P(lines),
        P(),
        P(None, "z", None, columns),
        P(None, "z", columns),
        P(None, "z", columns),
        P(None, "z", columns),
        P(None, "z", None, columns),
        P(None, "z", columns),
        P("z", columns),
        P(),
        P(),
        P(),
        P(),
        P(None, lines, None, None),
        P(None, lines, None, None),
        P(None, lines, None, None),
        P(None, lines, None, None),
    )
    return jax.shard_map(
        body, mesh=fine, in_specs=placed, out_specs=P(None, lines, None), check_vma=False
    )
```
